128 devices in a mesh: replica: 4 (over x), fsdp: 32 (over z, y, core).
Axes of the slice: x: 4, y: 4, z: 4, core: 2. Of those that a mesh axis runs over, the one named last changes fastest.
Arguments:
- gradients: bfloat16 [4, 8192, 8192], P('replica', 'fsdp'), may hold values from -0.3984375 to 0.3984375
- projection: bfloat16 [8192, 512], P('fsdp'), may hold values from -0.25 to 0.25
- plan: int32 [256], replicated, may hold values from 0 to 255, each once
- first_codes: bfloat16 [8192, 512], P(('replica', 'fsdp')), may hold values from -1 to 1
- first_scales: float32 [8192, 2], P(('replica', 'fsdp')), may hold values from 0.02 to 0.08
- second_codes: bfloat16 [8192, 512], P(('replica', 'fsdp')), may hold values from 0.099609375 to 1
- second_scales: float32 [8192, 2], P(('replica', 'fsdp')), may hold values from 0.0001 to 0.0004
Outputs:
- update: bfloat16 [8192, 8192], P('fsdp')
- new_first_codes: bfloat16 [8192, 512], P(('replica', 'fsdp'))
- new_first_scales: float32 [8192, 2], P(('replica', 'fsdp'))
- new_second_codes: bfloat16 [8192, 512], P(('replica', 'fsdp'))
- new_second_scales: float32 [8192, 2], P(('replica', 'fsdp'))
The draws below stay inside these ranges and needn't reach their ends.
Inputs may be any that keep to these rules, and one draw needn't show every extreme that they name: `plan`: each of the 256 panels appears once.
All inputs are finite; a program needn't handle non-finite values. Where the reference program divides by a largest or mean magnitude, that divisor is 1e-20 or more.
Results may differ from the reference program's by a relative error of at most 0.014.
Values may be sent and summed in bfloat16 or wider, within the bound.
A program may use at most 64 MiB of HBM per device.

```python
import math
import jax
import jax.numpy as jnp
from jax import lax

M = 8192
N = 8192
RANK = 512
PW = 32
QB = 256
STEP = 2
REPLICAS = 4
PANELS = 256
BLOCKS = 2


def levels(own_key, extent, cuts, smallest, high):
    def one(axis_at, blocks):
        heights = jax.random.uniform(jax.random.fold_in(jax.random.fold_in(own_key, 6), axis_at), (blocks,), jnp.float32, smallest / len(cuts), high / len(cuts))
        return jnp.repeat(jnp.exp(heights), extent[axis_at] // blocks).reshape((-1,) + (1,) * (len(extent) - axis_at - 1))

    gain = one(*cuts[0])
    for cut in cuts[1:]:
        gain = gain * one(*cut)
    return gain


def noise(rng, shape, spread, reach, cuts=(), kind=jnp.bfloat16):
    entries = jax.random.normal(rng, shape, jnp.float32) * spread
    if len(cuts) > 0:
        entries = levels(rng, shape, cuts, -0.22, 0.18) * entries
    return jnp.clip(entries, min=-reach, max=reach).astype(kind)


def setup_inputs(seed: int = 0) -> dict:
    arg_keys = jax.random.split(jax.random.key(seed), 8)
    return {
        "gradients": noise(arg_keys[0], (REPLICAS, M, N), 0.05, 0.3984375, ((0, 4), (1, 32))),
        "projection": noise(arg_keys[1], (M, RANK), RANK ** -0.5, 0.25, ((0, 32),)),
        "plan": jax.random.permutation(arg_keys[2], PANELS).astype(jnp.int32),
        "first_codes": jnp.clip(jax.random.uniform(arg_keys[3], (N, RANK), jnp.float32, -1.0, 1.0) * levels(arg_keys[3], (N, RANK), ((0, 128),), -0.4, 0.0), -1.0, 1.0).astype(jnp.bfloat16),
        "first_scales": jnp.clip(jnp.exp(math.log(0.08) - 1.3862944 * jax.random.uniform(arg_keys[4], (N, BLOCKS), jnp.float32) ** levels(arg_keys[4], (N, BLOCKS), ((0, 128),), -0.2, 0.2)), 0.02, 0.08),
        "second_codes": jnp.clip(0.099609375 + 0.9003906 * jax.random.uniform(arg_keys[5], (N, RANK), jnp.float32) ** levels(arg_keys[5], (N, RANK), ((0, 128),), -0.2, 0.2), 0.099609375, 1.0).astype(jnp.bfloat16),
        "second_scales": jnp.clip(jnp.exp(math.log(0.0004) - 1.3862944 * jax.random.uniform(arg_keys[6], (N, BLOCKS), jnp.float32) ** levels(arg_keys[6], (N, BLOCKS), ((0, 128),), -0.2, 0.2)), 0.0001, 0.0004),
    }


beta_one = 0.9
beta_two = 0.999
adam_eps = 1e-08
scale_eps = 1e-06

def expand(code_vals, scales):
    blocks = code_vals.astype(jnp.float32).reshape(code_vals.shape[0], -1, QB)
    return (blocks * scales[:, :, None]).reshape(code_vals.shape)

def requant(values):
    blocks = values.reshape(values.shape[0], -1, QB)
    peak = lax.optimization_barrier(jnp.max(jnp.abs(blocks), axis=2)) + scale_eps
    return ((blocks / peak[:, :, None]).reshape(values.shape).astype(jnp.bfloat16), peak)

def reference(gradients, projection, plan, first_codes, first_scales, second_codes, second_scales):
    summed = lax.optimization_barrier(jnp.sum(gradients.astype(jnp.float32), axis=0))
    column_ids = (plan[:, None] * PW + jnp.arange(PW, dtype=jnp.int32)[None, :]).reshape(-1).astype(jnp.int32)
    picked = jnp.take(summed, column_ids, axis=1)
    lowrank = lax.dot_general(picked, projection.astype(jnp.float32), (((0,), (0,)), ((), ())), precision=lax.Precision.HIGHEST)
    first = expand(first_codes, first_scales)
    second = expand(second_codes, second_scales)
    first_new = beta_one * first + (1.0 - beta_one) * lowrank
    second_new = beta_two * second + (1.0 - beta_two) * lowrank * lowrank
    corr_one = 1.0 - beta_one ** STEP
    corr_two = 1.0 - beta_two ** STEP
    direction = (first_new / corr_one / (jnp.sqrt(second_new / corr_two) + adam_eps)).astype(jnp.bfloat16)
    first_out, first_peak = requant(first_new)
    second_out, second_peak = requant(second_new)
    natural = jnp.zeros((N, RANK), jnp.bfloat16).at[column_ids].set(direction)
    update = lax.dot_general(projection, natural, (((1,), (1,)), ((), ())), preferred_element_type=jnp.float32).astype(jnp.bfloat16)
    return (update, first_out, first_peak, second_out, second_peak)
```

```python
import functools

import jax
import jax.numpy as jnp
from jax import lax
from jax.experimental import pallas as pl
from jax.experimental.pallas import tpu as pltpu
from jax.sharding import PartitionSpec as P

PW = 32
QB = 256
STEP = 2
RING = 4
LANES = 128

beta_one = 0.9
beta_two = 0.999
adam_eps = 1e-08
scale_eps = 1e-06

MESH = pl.DeviceIdType.MESH

CHIPS = RING**3
OWNED = 64
RANK = 512
PARTS = (
    (("x", "y", "z"), 96, 0),
    (("y", "z", "x"), 96, 96 * CHIPS),
    (("z", "x", "y"), 64, 192 * CHIPS),
)
HALF_ROWS = 256 * CHIPS


def block_row(part, chip):
    order, size, base = PARTS[part]
    a, b, c = (chip[name] for name in order)
    return base + ((a * RING + b) * RING + c) * size


def shifted(chip, axis, step):
    moved = dict(chip)
    moved[axis] = lax.rem(chip[axis] + step, RING)
    return moved


def device_of(chip, core):
    return (chip["x"], (chip["z"] * RING + chip["y"]) * 2 + core)


def rows(start, size):
    return pl.ds(pl.multiple_of(start, 32), size)


def owner_tiles(part):
    if part == 2:
        return [(slice(0, 64), slice(256, 384))]
    lanes = slice(part * 128, part * 128 + 128)
    return [(slice(0, 64), lanes), (slice(32 * part, 32 * part + 32), slice(384, 512))]


def put_block(ref, start, part, value, row_base=0):
    at = 0
    for row, lane in owner_tiles(part):
        size = row.stop - row.start
        ref[rows(start + at, size), :] = value[row_base + row.start : row_base + row.stop, lane].astype(ref.dtype)
        at += size


def kernel(
    plan_ref, table_ref, grad_hbm, proj_ref, fc_ref, fs_ref, sc_ref, ss_ref,
    update_hbm, ofc_ref, ofs_ref, osc_ref, oss_ref,
    grad_ref, turned, other_out, other_in, own_rows, proj_other,
    sums1, recv1, sums2, recv2, sums3, recv3, lowrank, whole, natural, update_ref,
    grad_sem, pair_send, pair_recv, rs_send, rs_recv, ag_send, ag_recv, fwd_send, fwd_recv, out_sem,
):
    replica = lax.axis_index("replica")
    inner = lax.axis_index("fsdp")
    chip = {"x": replica, "z": inner // 8, "y": lax.rem(inner // 2, RING)}
    core = lax.rem(inner, 2)
    other = 1 - core
    sibling = device_of(chip, other)
    cols = grad_hbm.shape[2] // RING

    loads = []
    for j in range(RING):
        loads.append(
            pltpu.make_async_copy(
                grad_hbm.at[0, :, pl.ds(j * cols, cols)], grad_ref.at[:, pl.ds(j * cols, cols)], grad_sem.at[j]
            )
        )
        loads[-1].start()

    barrier = pltpu.get_barrier_semaphore()
    pl.semaphore_signal(barrier, inc=1, device_id=sibling, device_id_type=MESH)
    for axis in ("x", "y", "z"):
        for step in range(1, RING):
            pl.semaphore_signal(
                barrier, inc=1, device_id=device_of(shifted(chip, axis, step), core), device_id_type=MESH
            )

    for j in range(RING):
        loads[j].wait()

        @pl.loop(0, cols // 256)
        def _(t, j=j):
            at = pl.multiple_of(j * cols + t * 256, 256)
            block = grad_ref[:, pl.ds(at, 256)].T
            turned[pl.ds(at // PW, 256 // PW)] = block.reshape(256 // PW, PW, block.shape[1])

    pl.semaphore_wait(barrier, 3 * (RING - 1) + 1)

    def remote(src, dst, send, recv, target):
        return pltpu.make_async_remote_copy(
            src_ref=src, dst_ref=dst, send_sem=send, recv_sem=recv, device_id=target, device_id_type=MESH
        )

    proj_copy = remote(proj_ref, proj_other, pair_send.at[RING], pair_recv.at[RING], sibling)
    proj_copy.start()

    def pick(target, which, first):
        @pl.loop(0, 32)
        def _(t):
            panel = first * 32 + t
            position = (panel // 2) * 4 + which * 2 + lax.rem(panel, 2)
            target[rows(panel * PW, PW), :] = turned[plan_ref[position]]

    pair = []
    span = CHIPS // RING * OWNED
    for j in range(RING):
        pick(other_out, other, j)
        part_rows = pl.ds(j * span, span)
        pair.append(
            remote(other_out.at[part_rows, :], other_in.at[part_rows, :], pair_send.at[j], pair_recv.at[j], sibling)
        )
        pair[-1].start()
    for j in range(RING):
        pick(own_rows, core, j)

    proj_copy.wait_recv()
    for j in range(RING):
        pair[j].wait_recv()

        @pl.loop(0, RING)
        def _(z, j=j):
            at = rows((j * RING + z) * RING * OWNED, RING * OWNED)
            product = jnp.dot(own_rows[at, :], proj_ref[...], preferred_element_type=jnp.float32)
            product += jnp.dot(other_in[at, :], proj_other[...], preferred_element_type=jnp.float32)
            for y in range(RING):
                for part in range(3):
                    put_block(sums1, block_row(part, {"x": j, "z": z, "y": y}), part, product, y * OWNED)

    def stage_copies(stage, source, landing, send, recv):
        copies = {}
        for part, (order, size, base) in enumerate(PARTS):
            unit = size * RING ** (2 - stage)
            origin = base // RING**stage
            landing_origin = 3 * base // RING ** (stage + 1)
            for step in range(1, RING):
                to = shifted(chip, order[stage], step)
                sem = stage * 9 + part * 3 + step - 1
                copies[part, step] = remote(
                    source.at[rows(origin + to[order[stage]] * unit, unit), :],
                    landing.at[pl.ds(landing_origin + (step - 1) * unit, unit), :],
                    send.at[sem],
                    recv.at[sem],
                    device_of(to, core),
                )
        return copies

    stages = [
        stage_copies(0, sums1, recv1, rs_send, rs_recv),
        stage_copies(1, sums2, recv2, rs_send, rs_recv),
        stage_copies(2, sums3, recv3, rs_send, rs_recv),
    ]
    sources = (sums1, sums2, sums3)
    landings = (recv1, recv2, recv3)

    for step in (2, 1, 3):
        for part in range(3):
            stages[0][part, step].start()

    for stage in (0, 1):
        for part, (order, size, base) in enumerate(PARTS):
            for step in range(1, RING):
                stages[stage][part, step].wait_recv()
            unit = size * RING ** (2 - stage)
            inner_unit = unit // RING
            own = base // RING**stage + chip[order[stage]] * unit
            landed = 3 * base // RING ** (stage + 1)
            target = base // RING ** (stage + 1)
            for step in (2, 1, 3, 0):
                slot = lax.rem(chip[order[stage + 1]] + step, RING)
                tile = min(inner_unit, 128 if size == 64 else 96)

                @pl.loop(0, inner_unit // tile)
                def _(t, own=own, landed=landed, target=target, slot=slot, unit=unit, inner_unit=inner_unit,
                      tile=tile, stage=stage):
                    at = slot * inner_unit + t * tile
                    total = sources[stage][rows(own + at, tile), :].astype(jnp.float32)
                    for i in range(3):
                        total += landings[stage][rows(landed + i * unit + at, tile), :].astype(jnp.float32)
                    sources[stage + 1][rows(target + at, tile), :] = total.astype(jnp.bfloat16)

                if step:
                    stages[stage + 1][part, step].start()

    for part, (order, size, base) in enumerate(PARTS):
        for step in range(1, RING):
            stages[2][part, step].wait_recv()
        total = sums3[rows(base // 16 + chip[order[2]] * size, size), :].astype(jnp.float32)
        for i in range(3):
            total += recv3[pl.ds(3 * base // 64 + i * size, size), :].astype(jnp.float32)
        at = 0
        for row, lane in owner_tiles(part):
            count = row.stop - row.start
            lowrank[row, lane] = total[at : at + count, :]
            at += count

    directions = []
    for b in range(RANK // QB):
        lane = slice(b * QB, (b + 1) * QB)
        low = lowrank[:, lane]
        first = fc_ref[:, lane].astype(jnp.float32) * fs_ref[:, b : b + 1]
        second = sc_ref[:, lane].astype(jnp.float32) * ss_ref[:, b : b + 1]
        first_new = beta_one * first + (1.0 - beta_one) * low
        second_new = beta_two * second + (1.0 - beta_two) * low * low
        corr_one = 1.0 - beta_one**STEP
        corr_two = 1.0 - beta_two**STEP
        directions.append(
            (first_new / corr_one / (jnp.sqrt(second_new / corr_two) + adam_eps)).astype(jnp.bfloat16)
        )
        for value, codes, scales in ((first_new, ofc_ref, ofs_ref), (second_new, osc_ref, oss_ref)):
            peak = jnp.max(jnp.abs(value), axis=1, keepdims=True) + scale_eps
            codes[:, lane] = (value / peak).astype(jnp.bfloat16)
            scales[:, b : b + 1] = peak
    direction = jnp.concatenate(directions, axis=1)

    mine = core * HALF_ROWS

    def in_whole(start, size):
        return pl.ds(start // PW, size // PW)

    for part in range(3):
        at = mine + block_row(part, chip)
        for row, lane in owner_tiles(part):
            size = row.stop - row.start
            whole[in_whole(at, size)] = direction[row, lane].reshape(size // PW, PW, LANES)
            at += size

    gathers, forwards = {}, []

    def forward(part, index, start, size):
        where = whole.at[in_whole(start, size)]
        forwards.append(
            remote(where, where, fwd_send.at[part * 7 + index], fwd_recv.at[part * 7 + index], sibling)
        )
        forwards[-1].start()

    def stage_start(part, stage):
        order, size, base = PARTS[part]
        unit = size * RING ** (2 - stage)
        at = dict(chip)
        for name in order[stage + 1 :]:
            at[name] = 0
        where = whole.at[in_whole(mine + block_row(part, at), unit)]
        for step in (2, 1, 3):
            sem = stage * 9 + part * 3 + step - 1
            gathers[part, stage, step] = remote(
                where, where, ag_send.at[sem], ag_recv.at[sem], device_of(shifted(chip, order[stage], step), core)
            )
            gathers[part, stage, step].start()

    def stage_landed(part, stage, step):
        order, size, base = PARTS[part]
        unit = size * RING ** (2 - stage)
        at = shifted(chip, order[stage], RING - step)
        for name in order[stage + 1 :]:
            at[name] = 0
        start = mine + block_row(part, at)
        where = whole.at[in_whole(start, unit)]
        sem = stage * 9 + part * 3 + step - 1
        remote(where, where, ag_send.at[sem], ag_recv.at[sem], sibling).wait_recv()
        return start, unit

    for part in range(3):
        stage_start(part, 2)
    for part in range(3):
        order, size, base = PARTS[part]
        for step in range(1, RING):
            stage_landed(part, 2, step)
        stage_start(part, 1)
        at = dict(chip)
        at[order[2]] = 0
        forward(part, 0, mine + block_row(part, at), size * RING)
    for part in range(3):
        landed = [stage_landed(part, 1, step) for step in range(1, RING)]
        stage_start(part, 0)
        for i, (start, unit) in enumerate(landed):
            forward(part, 1 + i, start, unit)
    for step in (1, 3, 2):
        for part in range(3):
            start, unit = stage_landed(part, 0, step)
            forward(part, 3 + step, start, unit)
    theirs = other * HALF_ROWS
    for part, (order, size, base) in enumerate(PARTS):
        at = dict(chip)
        at[order[2]] = 0
        waits = [(0, at, size * RING)]
        for step in range(1, RING):
            at = shifted(chip, order[1], RING - step)
            at[order[2]] = 0
            waits.append((step, at, size * RING))
            at = shifted(chip, order[0], RING - step)
            at[order[1]] = 0
            at[order[2]] = 0
            waits.append((3 + step, at, size * RING * RING))
        for index, at, unit in waits:
            where = whole.at[in_whole(theirs + block_row(part, at), unit)]
            sem = part * 7 + index
            remote(where, where, fwd_send.at[sem], fwd_recv.at[sem], sibling).wait_recv()

    tile = 512
    steps = update_ref.shape[1] // tile

    @pl.loop(0, steps)
    def _(t):
        for p in range(tile // PW):
            for lane in range(4):
                source = table_ref[lane * 256 + t * (tile // PW) + p]
                natural[p * PW : (p + 1) * PW, lane * LANES : (lane + 1) * LANES] = whole[source]
        product = lax.dot_general(
            proj_ref[...], natural[...], (((1,), (1,)), ((), ())), preferred_element_type=jnp.float32
        )
        update_ref[:, pl.ds(pl.multiple_of(t * tile, tile), tile)] = product.astype(jnp.bfloat16)

    store = pltpu.make_async_copy(update_ref, update_hbm, out_sem)
    store.start()

    proj_copy.wait_send()
    for copy in pair:
        copy.wait_send()
    for stage in stages:
        for copy in stage.values():
            copy.wait_send()
    for copy in gathers.values():
        copy.wait_send()
    for copy in forwards:
        copy.wait_send()
    store.wait()


def local(gradients, projection, plan, first_codes, first_scales, second_codes, second_scales):
    panel_count = plan.shape[0]
    position = jnp.arange(panel_count, dtype=jnp.int32)
    owner = position // 2
    half = position % 2
    chip = {"x": owner // 32, "z": owner // 8 % RING, "y": owner // 2 % RING}
    base = (owner % 2) * HALF_ROWS
    starts = [base + block_row(part, chip) for part in range(3)]
    table = jnp.stack(
        [start + half * PW for start in starts] + [jnp.where(half == 0, starts[0], starts[1]) + 64]
    )
    found = plan[None, :] == position[:, None]
    table = jnp.sum(jnp.where(found[None], table[:, None, :] // PW, 0), axis=2).reshape(-1)

    bf16, f32 = jnp.bfloat16, jnp.float32
    vmem = pl.BlockSpec(memory_space=pltpu.VMEM)
    smem = pl.BlockSpec(memory_space=pltpu.SMEM)
    hbm = pl.BlockSpec(memory_space=pl.ANY)
    sem = pltpu.SemaphoreType.DMA
    rows_count, col_count = gradients.shape[1:]
    half_cols = col_count // 2
    return pl.pallas_call(
        kernel,
        out_shape=(
            jax.ShapeDtypeStruct((rows_count, col_count), bf16),
            jax.ShapeDtypeStruct(first_codes.shape, bf16),
            jax.ShapeDtypeStruct(first_scales.shape, f32),
            jax.ShapeDtypeStruct(second_codes.shape, bf16),
            jax.ShapeDtypeStruct(second_scales.shape, f32),
        ),
        in_specs=[smem, smem, hbm, vmem, vmem, vmem, vmem, vmem],
        out_specs=(hbm, vmem, vmem, vmem, vmem),
        scratch_shapes=[
            pltpu.VMEM((rows_count, col_count), bf16),
            pltpu.VMEM((col_count // PW, PW, rows_count), bf16),
            pltpu.VMEM((half_cols, rows_count), bf16),
            pltpu.VMEM((half_cols, rows_count), bf16),
            pltpu.VMEM((half_cols, rows_count), bf16),
            pltpu.VMEM(projection.shape, bf16),
            pltpu.VMEM((HALF_ROWS, LANES), bf16),
            pltpu.VMEM((HALF_ROWS * 3 // 4, LANES), bf16),
            pltpu.VMEM((HALF_ROWS // 4, LANES), bf16),
            pltpu.VMEM((HALF_ROWS * 3 // 16, LANES), bf16),
            pltpu.VMEM((HALF_ROWS // 16, LANES), bf16),
            pltpu.VMEM((HALF_ROWS * 3 // 64, LANES), bf16),
            pltpu.VMEM(first_codes.shape, f32),
            pltpu.VMEM((2 * HALF_ROWS // PW, PW, LANES), bf16),
            pltpu.VMEM((512, RANK), bf16),
            pltpu.VMEM((rows_count, col_count), bf16),
            sem((4,)), sem((5,)), sem((5,)), sem((27,)), sem((27,)), sem((27,)), sem((27,)), sem((21,)), sem((21,)),
            sem,
        ],
        compiler_params=pltpu.CompilerParams(
            collective_id=0, has_side_effects=True, vmem_limit_bytes=60 * 1024 * 1024
        ),
    )(plan, table, gradients, projection, first_codes, first_scales, second_codes, second_scales)


def solution(mesh):
    in_specs = (
        P("replica", "fsdp", None),
        P("fsdp", None),
        P(),
        P(("replica", "fsdp"), None),
        P(("replica", "fsdp"), None),
        P(("replica", "fsdp"), None),
        P(("replica", "fsdp"), None),
    )
    out_specs = (
        P("fsdp", None),
        P(("replica", "fsdp"), None),
        P(("replica", "fsdp"), None),
        P(("replica", "fsdp"), None),
        P(("replica", "fsdp"), None),
    )
    return jax.shard_map(local, mesh=mesh, in_specs=in_specs, out_specs=out_specs, check_vma=False)
```

```python
import functools

import jax
import jax.numpy as jnp
from jax import lax
from jax.experimental import pallas as pl
from jax.experimental.pallas import tpu as pltpu
from jax.sharding import PartitionSpec as P

PW = 32
QB = 256
STEP = 2
RING = 4
LANES = 128

beta_one = 0.9
beta_two = 0.999
adam_eps = 1e-08
scale_eps = 1e-06

MESH = pl.DeviceIdType.MESH

CHIPS = RING**3
OWNED = 64
RANK = 512
PARTS = (
    (("x", "y", "z"), 96, 0),
    (("y", "z", "x"), 96, 96 * CHIPS),
    (("z", "x", "y"), 64, 192 * CHIPS),
)
HALF_ROWS = 256 * CHIPS
RS_SETS = ((1, 0), (2, 3))
AG_SETS = ((0, 1), (3, 2))


def block_row(part, chip):
    order, size, base = PARTS[part]
    a, b, c = (chip[name] for name in order)
    return base + ((a * RING + b) * RING + c) * size


def shifted(chip, axis, step):
    moved = dict(chip)
    moved[axis] = lax.rem(chip[axis] + step, RING)
    return moved


def device_of(chip, core):
    return (chip["x"], (chip["z"] * RING + chip["y"]) * 2 + core)


def rows(start, size):
    return pl.ds(pl.multiple_of(start, 32), size)


def owner_tiles(part):
    if part == 2:
        return [(slice(0, 64), slice(256, 384))]
    lanes = slice(part * 128, part * 128 + 128)
    return [(slice(0, 64), lanes), (slice(32 * part, 32 * part + 32), slice(384, 512))]


def put_block(ref, start, part, value, row_base=0):
    at = 0
    for row, lane in owner_tiles(part):
        size = row.stop - row.start
        ref[rows(start + at, size), :] = value[row_base + row.start : row_base + row.stop, lane].astype(ref.dtype)
        at += size


def kernel(
    plan_ref, table_ref, grad_hbm, proj_ref, fc_ref, fs_ref, sc_ref, ss_ref,
    update_hbm, ofc_ref, ofs_ref, osc_ref, oss_ref,
    grad_ref, turned, other_out, other_in, own_rows, proj_other,
    sums1, transit, recv1, sums2, recv2, sums3, recv3, lowrank, whole, natural, update_ref,
    grad_sem, pair_send, pair_recv, first_send, first_recv, rs_send, rs_recv, near_send, near_recv, ag_send, ag_recv, fwd_send, fwd_recv, out_sem,
):
    replica = lax.axis_index("replica")
    inner = lax.axis_index("fsdp")
    chip = {"x": replica, "z": inner // 8, "y": lax.rem(inner // 2, RING)}
    core = lax.rem(inner, 2)
    other = 1 - core
    sibling = device_of(chip, other)
    cols = grad_hbm.shape[2] // RING

    loads = []
    for j in range(RING):
        loads.append(
            pltpu.make_async_copy(
                grad_hbm.at[0, :, pl.ds(j * cols, cols)], grad_ref.at[:, pl.ds(j * cols, cols)], grad_sem.at[j]
            )
        )
        loads[-1].start()

    barrier = pltpu.get_barrier_semaphore()
    pl.semaphore_signal(barrier, inc=1, device_id=sibling, device_id_type=MESH)
    for axis in ("x", "y", "z"):
        for step in range(1, RING):
            pl.semaphore_signal(
                barrier, inc=1, device_id=device_of(shifted(chip, axis, step), core), device_id_type=MESH
            )

    for j in range(RING):
        loads[j].wait()

        @pl.loop(0, cols // 256)
        def _(t, j=j):
            at = pl.multiple_of(j * cols + t * 256, 256)
            block = grad_ref[:, pl.ds(at, 256)].T
            turned[pl.ds(at // PW, 256 // PW)] = block.reshape(256 // PW, PW, block.shape[1])

    pl.semaphore_wait(barrier, 3 * (RING - 1) + 1)

    def remote(src, dst, send, recv, target):
        return pltpu.make_async_remote_copy(
            src_ref=src, dst_ref=dst, send_sem=send, recv_sem=recv, device_id=target, device_id_type=MESH
        )

    proj_copy = remote(proj_ref, proj_other, pair_send.at[RING], pair_recv.at[RING], sibling)
    proj_copy.start()

    def pick(target, which, first):
        @pl.loop(0, 32)
        def _(t):
            panel = first * 32 + t
            position = (panel // 2) * 4 + which * 2 + lax.rem(panel, 2)
            target[rows(panel * PW, PW), :] = turned[plan_ref[position]]

    pair = []
    span = CHIPS // RING * OWNED
    for j in range(RING):
        pick(other_out, other, j)
        part_rows = pl.ds(j * span, span)
        pair.append(
            remote(other_out.at[part_rows, :], other_in.at[part_rows, :], pair_send.at[j], pair_recv.at[j], sibling)
        )
        pair[-1].start()
    for j in range(RING):
        pick(own_rows, core, j)

    proj_copy.wait_recv()
    for j in range(RING):
        pair[j].wait_recv()

        @pl.loop(0, RING)
        def _(z, j=j):
            at = rows((j * RING + z) * RING * OWNED, RING * OWNED)
            product = jnp.dot(own_rows[at, :], proj_ref[...], preferred_element_type=jnp.float32)
            product += jnp.dot(other_in[at, :], proj_other[...], preferred_element_type=jnp.float32)
            for y in range(RING):
                for part in range(3):
                    put_block(sums1, block_row(part, {"x": j, "z": z, "y": y}), part, product, y * OWNED)

    def sub_row(part, a, b):
        order, size, base = PARTS[part]
        return block_row(part, {order[0]: a, order[1]: b, order[2]: 0})

    opening = {}
    for k in range(2):
        for part, (order, size, base) in enumerate(PARTS):
            a, b = chip[order[0]], chip[order[1]]
            sub = size * RING
            for way, flow in enumerate((1, RING - 1)):
                off = RS_SETS[way][k]
                b_to = lax.rem(b + off, RING)
                onward = device_of(shifted(chip, order[0], flow), core)
                backward = device_of(shifted(chip, order[0], RING - flow), core)
                sem = part * 4 + way * 2 + k
                slot = base // 4 + (way * 2 + k) * sub
                land = base // 2 + off * 2 * sub
                opening["far", part, way, k] = remote(
                    sums1.at[rows(sub_row(part, lax.rem(a + 2, RING), b_to), sub), :],
                    transit.at[pl.ds(slot, sub), :],
                    first_send.at[sem], first_recv.at[sem], onward,
                )
                opening["raw", part, way, k] = remote(
                    sums1.at[rows(sub_row(part, lax.rem(a + RING - flow, RING), b_to), sub), :],
                    recv1.at[pl.ds(land, sub), :],
                    first_send.at[12 + sem], first_recv.at[12 + sem], backward,
                )
                opening["both", part, way, k] = remote(
                    sums1.at[rows(sub_row(part, lax.rem(a + flow, RING), b_to), sub), :],
                    recv1.at[pl.ds(land + sub, sub), :],
                    first_send.at[24 + sem], first_recv.at[24 + sem], onward,
                )

    def first_start(kind, k):
        for part in range(3):
            for way in range(2):
                opening[kind, part, way, k].start()

    first_start("far", 0)
    first_start("far", 1)
    for k in range(2):
        first_start("raw", k)
        for part, (order, size, base) in enumerate(PARTS):
            for way, flow in enumerate((1, RING - 1)):
                opening["far", part, way, k].wait_recv()
                own = sub_row(
                    part,
                    lax.rem(chip[order[0]] + flow, RING),
                    lax.rem(chip[order[1]] + RS_SETS[way][k], RING),
                )
                slot = base // 4 + (way * 2 + k) * size * RING

                @pl.loop(0, RING)
                def _(t, own=own, slot=slot, size=size):
                    at = rows(own + t * size, size)
                    total = sums1[at, :].astype(jnp.float32)
                    total += transit[rows(slot + t * size, size), :].astype(jnp.float32)
                    sums1[at, :] = total.astype(jnp.bfloat16)

                opening["both", part, way, k].start()

    def stage_copies(stage, source, landing):
        copies = {}
        for part, (order, size, base) in enumerate(PARTS):
            unit = size * RING ** (2 - stage)
            origin = base // RING**stage
            landing_origin = 3 * base // RING ** (stage + 1)
            for step in range(1, RING):
                to = shifted(chip, order[stage], step)
                sem = (stage - 1) * 9 + part * 3 + step - 1
                copies[part, step] = remote(
                    source.at[rows(origin + to[order[stage]] * unit, unit), :],
                    landing.at[pl.ds(landing_origin + (step - 1) * unit, unit), :],
                    rs_send.at[sem],
                    rs_recv.at[sem],
                    device_of(to, core),
                )
        return copies

    middle, closing = stage_copies(1, sums2, recv2), stage_copies(2, sums3, recv3)

    for k in range(2):
        for part, (order, size, base) in enumerate(PARTS):
            a, b = chip[order[0]], chip[order[1]]
            sub = size * RING
            for way in range(2):
                off = RS_SETS[way][k]
                b_to = lax.rem(b + off, RING)
                own = sub_row(part, a, b_to)
                land = base // 2 + off * 2 * sub
                target = base // RING + b_to * sub
                opening["raw", part, way, k].wait_recv()
                opening["both", part, way, k].wait_recv()

                @pl.loop(0, RING)
                def _(t, own=own, land=land, target=target, sub=sub, size=size):
                    total = sums1[rows(own + t * size, size), :].astype(jnp.float32)
                    total += recv1[rows(land + t * size, size), :].astype(jnp.float32)
                    total += recv1[rows(land + sub + t * size, size), :].astype(jnp.float32)
                    sums2[rows(target + t * size, size), :] = total.astype(jnp.bfloat16)

                if off:
                    middle[part, off].start()

    for part, (order, size, base) in enumerate(PARTS):
        for step in range(1, RING):
            middle[part, step].wait_recv()
        unit = size * RING
        own = base // RING + chip[order[1]] * unit
        landed = 3 * base // RING**2
        target = base // RING**2
        for step in (2, 1, 3, 0):
            at = lax.rem(chip[order[2]] + step, RING) * size
            total = sums2[rows(own + at, size), :].astype(jnp.float32)
            for i in range(3):
                total += recv2[rows(landed + i * unit + at, size), :].astype(jnp.float32)
            sums3[rows(target + at, size), :] = total.astype(jnp.bfloat16)
            if step:
                closing[part, step].start()

    for part, (order, size, base) in enumerate(PARTS):
        for step in range(1, RING):
            closing[part, step].wait_recv()
        total = sums3[rows(base // 16 + chip[order[2]] * size, size), :].astype(jnp.float32)
        for i in range(3):
            total += recv3[pl.ds(3 * base // 64 + i * size, size), :].astype(jnp.float32)
        at = 0
        for row, lane in owner_tiles(part):
            count = row.stop - row.start
            lowrank[row, lane] = total[at : at + count, :]
            at += count

    first_scales, second_scales = fs_ref[...].T, ss_ref[...].T
    directions, peaks = [], []
    for b in range(RANK // QB):
        lane = slice(b * QB, (b + 1) * QB)
        low = lowrank[:, lane]
        first = fc_ref[:, lane].astype(jnp.float32) * first_scales[:, b : b + 1]
        second = sc_ref[:, lane].astype(jnp.float32) * second_scales[:, b : b + 1]
        first_new = beta_one * first + (1.0 - beta_one) * low
        second_new = beta_two * second + (1.0 - beta_two) * low * low
        corr_one = 1.0 - beta_one**STEP
        corr_two = 1.0 - beta_two**STEP
        directions.append(
            (first_new / corr_one / (jnp.sqrt(second_new / corr_two) + adam_eps)).astype(jnp.bfloat16)
        )
        for value, codes in ((first_new, ofc_ref), (second_new, osc_ref)):
            peak = jnp.max(jnp.abs(value), axis=1, keepdims=True) + scale_eps
            codes[:, lane] = (value / peak).astype(jnp.bfloat16)
            peaks.append(peak)
    direction = jnp.concatenate(directions, axis=1)
    ofs_ref[...] = jnp.concatenate(peaks[0::2], axis=1).T
    oss_ref[...] = jnp.concatenate(peaks[1::2], axis=1).T

    mine = core * HALF_ROWS

    def in_whole(start, size):
        return pl.ds(start // PW, size // PW)

    for part in range(3):
        at = mine + block_row(part, chip)
        for row, lane in owner_tiles(part):
            size = row.stop - row.start
            whole[in_whole(at, size)] = direction[row, lane].reshape(size // PW, PW, LANES)
            at += size

    started, forwards = [], []

    def copy_of(start, size, send, recv, target):
        where = whole.at[in_whole(start, size)]
        return remote(where, where, send, recv, target)

    def spread(start, size, send, recv, target):
        started.append(copy_of(mine + start, size, send, recv, target))
        started[-1].start()

    def forward(start, size):
        index = len(forwards)
        forwards.append((start, size))
        spread(start, size, fwd_send.at[index], fwd_recv.at[index], sibling)

    def landed(start, size, recv):
        copy_of(mine + start, size, first_send.at[0], recv, sibling).wait_recv()
        return start, size

    def sub_of(part, a_off, off):
        order, size, base = PARTS[part]
        start = sub_row(
            part, lax.rem(chip[order[0]] + a_off, RING), lax.rem(chip[order[1]] + off, RING)
        )
        return start, size * RING

    def near_start(part, off):
        order = PARTS[part][0]
        for way, flow in enumerate((1, RING - 1)):
            sem = 12 * way + part * 4 + off
            to = device_of(shifted(chip, order[0], flow), core)
            spread(*sub_of(part, 0, off), near_send.at[sem], near_recv.at[sem], to)

    def near_landed(part, off):
        order = PARTS[part][0]
        for way, flow in enumerate((1, RING - 1)):
            piece = landed(*sub_of(part, RING - flow, off), near_recv.at[12 * way + part * 4 + off])
            if off in AG_SETS[way]:
                sem = 24 + part * 4 + off
                to = device_of(shifted(chip, order[0], flow), core)
                spread(*piece, near_send.at[sem], near_recv.at[sem], to)
            forward(*piece)

    for part, (order, size, base) in enumerate(PARTS):
        for step in (2, 1, 3):
            sem = 9 + part * 3 + step - 1
            to = device_of(shifted(chip, order[2], step), core)
            spread(block_row(part, chip), size, ag_send.at[sem], ag_recv.at[sem], to)
    for part, (order, size, base) in enumerate(PARTS):
        for step in range(1, RING):
            landed(block_row(part, shifted(chip, order[2], RING - step)), size, ag_recv.at[9 + part * 3 + step - 1])
        piece = sub_of(part, 0, 0)
        for step in (2, 1, 3):
            sem = part * 3 + step - 1
            spread(*piece, ag_send.at[sem], ag_recv.at[sem], device_of(shifted(chip, order[1], step), core))
        near_start(part, 0)
        forward(*piece)

    def second_landed(part, step):
        off = RING - step
        piece = landed(*sub_of(part, 0, off), ag_recv.at[part * 3 + step - 1])
        near_start(part, off)
        forward(*piece)

    for step in (1, 3):
        for part in range(3):
            second_landed(part, step)
    for part in range(3):
        near_landed(part, 0)
    for part in range(3):
        second_landed(part, 2)
    for off in (3, 1, 2):
        for part in range(3):
            near_landed(part, off)
    for off in (0, 3, 1, 2):
        for part in range(3):
            forward(*landed(*sub_of(part, 2, off), near_recv.at[24 + part * 4 + off]))
    theirs = other * HALF_ROWS
    for index, (start, size) in enumerate(forwards):
        copy_of(theirs + start, size, first_send.at[0], fwd_recv.at[index], sibling).wait_recv()

    tile = 512
    steps = update_ref.shape[1] // tile

    @pl.loop(0, steps)
    def _(t):
        for p in range(tile // PW):
            packed = table_ref[t * (tile // PW) + p]
            half = lax.shift_right_logical(packed, 30)
            starts = [lax.shift_right_logical(packed, 10 * part) & 1023 for part in range(3)]
            sources = [start + half for start in starts] + [starts[0] + 2 + half * (starts[1] - starts[0])]
            for lane, source in enumerate(sources):
                natural[p * PW : (p + 1) * PW, lane * LANES : (lane + 1) * LANES] = whole[source]
        product = lax.dot_general(
            proj_ref[...], natural[...], (((1,), (1,)), ((), ())), preferred_element_type=jnp.float32
        )
        update_ref[:, pl.ds(pl.multiple_of(t * tile, tile), tile)] = product.astype(jnp.bfloat16)

    store = pltpu.make_async_copy(update_ref, update_hbm, out_sem)
    store.start()

    proj_copy.wait_send()
    for copy in pair:
        copy.wait_send()
    for stage in (opening, middle, closing):
        for copy in stage.values():
            copy.wait_send()
    for copy in started:
        copy.wait_send()
    store.wait()


def local(gradients, projection, plan, first_codes, first_scales, second_codes, second_scales):
    panel_count = plan.shape[0]
    position = jnp.arange(panel_count, dtype=jnp.int32)
    owner = position // 2
    half = position % 2
    chip = {"x": owner // 32, "z": owner // 8 % RING, "y": owner // 2 % RING}
    base = (owner % 2) * HALF_ROWS
    starts = [base + block_row(part, chip) for part in range(3)]
    starts = [start // PW for start in starts]
    packed = starts[0] + starts[1] * 1024 + starts[2] * 1024 * 1024 + half * 1024 * 1024 * 1024
    found = plan[None, :] == position[:, None]
    table = jnp.sum(jnp.where(found, packed[None, :], 0), axis=1)

    bf16, f32 = jnp.bfloat16, jnp.float32
    vmem = pl.BlockSpec(memory_space=pltpu.VMEM)
    smem = pl.BlockSpec(memory_space=pltpu.SMEM)
    hbm = pl.BlockSpec(memory_space=pl.ANY)
    sem = pltpu.SemaphoreType.DMA
    rows_count, col_count = gradients.shape[1:]
    half_cols = col_count // 2
    update, first_out, first_peak, second_out, second_peak = pl.pallas_call(
        kernel,
        out_shape=(
            jax.ShapeDtypeStruct((rows_count, col_count), bf16),
            jax.ShapeDtypeStruct(first_codes.shape, bf16),
            jax.ShapeDtypeStruct(first_scales.shape[::-1], f32),
            jax.ShapeDtypeStruct(second_codes.shape, bf16),
            jax.ShapeDtypeStruct(second_scales.shape[::-1], f32),
        ),
        in_specs=[smem, smem, hbm, vmem, vmem, vmem, vmem, vmem],
        out_specs=(hbm, vmem, vmem, vmem, vmem),
        scratch_shapes=[
            pltpu.VMEM((rows_count, col_count), bf16),
            pltpu.VMEM((col_count // PW, PW, rows_count), bf16),
            pltpu.VMEM((half_cols, rows_count), bf16),
            pltpu.VMEM((half_cols, rows_count), bf16),
            pltpu.VMEM((half_cols, rows_count), bf16),
            pltpu.VMEM(projection.shape, bf16),
            pltpu.VMEM((HALF_ROWS, LANES), bf16),
            pltpu.VMEM((HALF_ROWS // 4, LANES), bf16),
            pltpu.VMEM((HALF_ROWS // 2, LANES), bf16),
            pltpu.VMEM((HALF_ROWS // 4, LANES), bf16),
            pltpu.VMEM((HALF_ROWS * 3 // 16, LANES), bf16),
            pltpu.VMEM((HALF_ROWS // 16, LANES), bf16),
            pltpu.VMEM((HALF_ROWS * 3 // 64, LANES), bf16),
            pltpu.VMEM(first_codes.shape, f32),
            pltpu.VMEM((2 * HALF_ROWS // PW, PW, LANES), bf16),
            pltpu.VMEM((512, RANK), bf16),
            pltpu.VMEM((rows_count, col_count), bf16),
            sem((4,)), sem((5,)), sem((5,)), sem((36,)), sem((36,)), sem((18,)), sem((18,)), sem((36,)), sem((36,)),
            sem((18,)), sem((18,)), sem((48,)), sem((48,)), sem,
        ],
        compiler_params=pltpu.CompilerParams(
            collective_id=0, has_side_effects=True, vmem_limit_bytes=60 * 1024 * 1024
        ),
    )(plan, table, gradients, projection, first_codes, first_scales.T, second_codes, second_scales.T)
    return update, first_out, first_peak.T, second_out, second_peak.T


def solution(mesh):
    in_specs = (
        P("replica", "fsdp", None),
        P("fsdp", None),
        P(),
        P(("replica", "fsdp"), None),
        P(("replica", "fsdp"), None),
        P(("replica", "fsdp"), None),
        P(("replica", "fsdp"), None),
    )
    out_specs = (
        P("fsdp", None),
        P(("replica", "fsdp"), None),
        P(("replica", "fsdp"), None),
        P(("replica", "fsdp"), None),
        P(("replica", "fsdp"), None),
    )
    return jax.shard_map(local, mesh=mesh, in_specs=in_specs, out_specs=out_specs, check_vma=False)
```

```python
import functools

import jax
import jax.numpy as jnp
from jax import lax
from jax.experimental import pallas as pl
from jax.experimental.pallas import tpu as pltpu
from jax.sharding import PartitionSpec as P

PW = 32
QB = 256
STEP = 2
RING = 4
LANES = 128

beta_one = 0.9
beta_two = 0.999
adam_eps = 1e-08
scale_eps = 1e-06

MESH = pl.DeviceIdType.MESH

CHIPS = RING**3
OWNED = 64
RANK = 512
HALF_ROWS = 256 * CHIPS
ORDERS = (("x", "y", "z"), ("y", "z", "x"), ("z", "x", "y"))
LANES_OF = (((0, 3), (1,), (2,)), ((0,), (1, 3), (2,)))
BOTH = [(half, part) for half in range(2) for part in range(3)]


def part_of(half, part):
    sizes = [PW * len(lanes) for lanes in LANES_OF[half]]
    return ORDERS[part], sizes[part], half * HALF_ROWS // 2 + sum(sizes[:part]) * CHIPS


def block_row(half, part, chip):
    order, size, base = part_of(half, part)
    a, b, c = (chip[name] for name in order)
    return base + ((a * RING + b) * RING + c) * size


def shifted(chip, axis, step):
    moved = dict(chip)
    moved[axis] = lax.rem(chip[axis] + step, RING)
    return moved


def device_of(chip, core):
    return (chip["x"], (chip["z"] * RING + chip["y"]) * 2 + core)


def rows(start, size):
    return pl.ds(pl.multiple_of(start, 32), size)


def lanes_at(block):
    return slice(block * LANES, (block + 1) * LANES)


def kernel(
    plan_ref, grad_hbm, proj_hbm, fc_hbm, fs_hbm, sc_hbm, ss_hbm,
    whole, ofc_ref, ofs_ref, osc_ref, oss_ref,
    proj_ref, fc_ref, fs_ref, sc_ref, ss_ref, grad_ref, turned, other_out, other_in, own_rows, proj_other,
    sums1, transit, recv1, sums2, recv2, sums3, recv3,
    grad_sem, small_sem, pair_send, pair_recv, first_send, first_recv, rs_send, rs_recv, near_send, near_recv, ag_send, ag_recv, fwd_send, fwd_recv,
):
    replica = lax.axis_index("replica")
    inner = lax.axis_index("fsdp")
    chip = {"x": replica, "z": inner // 8, "y": lax.rem(inner // 2, RING)}
    core = lax.rem(inner, 2)
    other = 1 - core
    sibling = device_of(chip, other)
    cols = grad_hbm.shape[2] // RING

    loads = []
    for j in range(RING):
        loads.append(
            pltpu.make_async_copy(
                grad_hbm.at[0, :, pl.ds(j * cols, cols)], grad_ref.at[:, pl.ds(j * cols, cols)], grad_sem.at[j]
            )
        )
        loads[-1].start()

    small = []
    for i, (source, target) in enumerate(
        ((proj_hbm, proj_ref), (fc_hbm, fc_ref), (fs_hbm, fs_ref), (sc_hbm, sc_ref), (ss_hbm, ss_ref))
    ):
        small.append(pltpu.make_async_copy(source, target, small_sem.at[i]))
        small[-1].start()

    barrier = pltpu.get_barrier_semaphore()
    pl.semaphore_signal(barrier, inc=1, device_id=sibling, device_id_type=MESH)
    for axis in ("x", "y", "z"):
        for step in range(1, RING):
            pl.semaphore_signal(
                barrier, inc=1, device_id=device_of(shifted(chip, axis, step), core), device_id_type=MESH
            )

    for j in range(RING):
        loads[j].wait()

        @pl.loop(0, cols // 256)
        def _(t, j=j):
            at = pl.multiple_of(j * cols + t * 256, 256)
            block = grad_ref[:, pl.ds(at, 256)].T
            turned[pl.ds(at // PW, 256 // PW)] = block.reshape(256 // PW, PW, block.shape[1])

    for copy in small:
        copy.wait()
    pl.semaphore_wait(barrier, 3 * (RING - 1) + 1)

    def remote(src, dst, send, recv, target):
        return pltpu.make_async_remote_copy(
            src_ref=src, dst_ref=dst, send_sem=send, recv_sem=recv, device_id=target, device_id_type=MESH
        )

    proj_copy = remote(proj_ref, proj_other, pair_send.at[2], pair_recv.at[2], sibling)
    proj_copy.start()

    span = CHIPS * PW

    def pick(target, which, half):
        @pl.loop(0, CHIPS)
        def _(t):
            target[rows(half * span + t * PW, PW), :] = turned[plan_ref[(t * 2 + which) * 2 + half]]

    pair = []
    for half in range(2):
        pick(other_out, other, half)
        part_rows = pl.ds(half * span, span)
        pair.append(
            remote(
                other_out.at[part_rows, :], other_in.at[part_rows, :],
                pair_send.at[half], pair_recv.at[half], sibling,
            )
        )
        pair[-1].start()

    def project(half):
        pick(own_rows, core, half)
        if half == 0:
            proj_copy.wait_recv()
        pair[half].wait_recv()

        @pl.loop(0, CHIPS // 8)
        def _(t):
            at = rows(half * span + t * 8 * PW, 8 * PW)
            product = jnp.dot(own_rows[at, :], proj_ref[...], preferred_element_type=jnp.float32)
            product += jnp.dot(other_in[at, :], proj_other[...], preferred_element_type=jnp.float32)
            for i in range(8):
                to = {"x": t // 2, "z": (t % 2) * 2 + i // 4, "y": i % 4}
                for part in range(3):
                    for j, block in enumerate(LANES_OF[half][part]):
                        sums1[rows(block_row(half, part, to) + j * PW, PW), :] = product[
                            i * PW : (i + 1) * PW, lanes_at(block)
                        ].astype(jnp.bfloat16)

    def sub_row(half, part, a, b):
        order = ORDERS[part]
        return block_row(half, part, {order[0]: a, order[1]: b, order[2]: 0})

    opening, middle, closing = {}, {}, {}
    for half, part in BOTH:
        order, size, base = part_of(half, part)
        a = chip[order[0]]
        message = 2 * size * RING
        for way, flow in enumerate((1, RING - 1)):
            onward = device_of(shifted(chip, order[0], flow), core)
            backward = device_of(shifted(chip, order[0], RING - flow), core)
            sem = half * 6 + part * 2 + way
            land = base // 2 + way * 2 * message
            for kind, (steps, landing, place, target) in enumerate(
                (
                    (2, transit, base // 4 + way * message, onward),
                    (RING - flow, recv1, land, backward),
                    (flow, recv1, land + message, onward),
                )
            ):
                opening[kind, half, part, way] = remote(
                    sums1.at[rows(sub_row(half, part, lax.rem(a + steps, RING), 2 * way), message), :],
                    landing.at[pl.ds(place, message), :],
                    first_send.at[12 * kind + sem], first_recv.at[12 * kind + sem], target,
                )
        for stage, source, landing, copies in ((1, sums2, recv2, middle), (2, sums3, recv3, closing)):
            unit = size * RING ** (2 - stage)
            origin = base // RING**stage
            for step in range(1, RING):
                to = shifted(chip, order[stage], step)
                sem = (stage - 1) * 18 + half * 9 + part * 3 + step - 1
                copies[half, part, step] = remote(
                    source.at[rows(origin + to[order[stage]] * unit, unit), :],
                    landing.at[pl.ds(3 * base // RING ** (stage + 1) + (step - 1) * unit, unit), :],
                    rs_send.at[sem], rs_recv.at[sem], device_of(to, core),
                )

    def opening_start(kind, half):
        for part in range(3):
            for way in range(2):
                opening[kind, half, part, way].start()

    def add(count, target, at, *terms):
        tile = 128

        @pl.loop(0, count // tile)
        def _(t):
            total = sum(ref[rows(row + t * tile, tile), :].astype(jnp.float32) for ref, row in terms)
            target[rows(at + t * tile, tile), :] = total.astype(jnp.bfloat16)

    def pass_on(half):
        for part in range(3):
            order, size, base = part_of(half, part)
            message = 2 * size * RING
            for way, flow in enumerate((1, RING - 1)):
                opening[0, half, part, way].wait_recv()
                own = sub_row(half, part, lax.rem(chip[order[0]] + flow, RING), 2 * way)
                add(message, sums1, own, (sums1, own), (transit, base // 4 + way * message))
                opening[2, half, part, way].start()

    def first_done(half):
        for part in range(3):
            order, size, base = part_of(half, part)
            message = 2 * size * RING
            for way in range(2):
                opening[1, half, part, way].wait_recv()
                opening[2, half, part, way].wait_recv()
                own = sub_row(half, part, chip[order[0]], 2 * way)
                land = base // 2 + way * 2 * message
                add(
                    message, sums2, base // RING + way * message,
                    (sums1, own), (recv1, land), (recv1, land + message),
                )
            for step in (2, 1, 3):
                middle[half, part, step].start()

    def middle_done(half):
        for part in range(3):
            order, size, base = part_of(half, part)
            for step in range(1, RING):
                middle[half, part, step].wait_recv()
            unit = size * RING
            own = base // RING + chip[order[1]] * unit
            landings = [(recv2, 3 * base // RING**2 + i * unit) for i in range(3)]
            add(unit, sums3, base // RING**2, (sums2, own), *landings)
            for step in (2, 1, 3):
                closing[half, part, step].start()

    first_scales, second_scales = fs_ref[...].T, ss_ref[...].T
    peaks = ([], [])

    def adam(half):
        low = {}
        for part in range(3):
            order, size, base = part_of(half, part)
            for step in range(1, RING):
                closing[half, part, step].wait_recv()
            total = sums3[rows(base // 16 + chip[order[2]] * size, size), :].astype(jnp.float32)
            for i in range(3):
                total += recv3[pl.ds(3 * base // 64 + i * size, size), :].astype(jnp.float32)
            for j, block in enumerate(LANES_OF[half][part]):
                low[block] = total[j * PW : (j + 1) * PW, :]
        row = slice(half * PW, (half + 1) * PW)
        mine_peaks = ([], [])
        direction = {}
        for b in range(RANK // QB):
            lane = slice(b * QB, (b + 1) * QB)
            lowrank = jnp.concatenate([low[2 * b], low[2 * b + 1]], axis=1)
            first = fc_ref[row, lane].astype(jnp.float32) * first_scales[row, b : b + 1]
            second = sc_ref[row, lane].astype(jnp.float32) * second_scales[row, b : b + 1]
            first_new = beta_one * first + (1.0 - beta_one) * lowrank
            second_new = beta_two * second + (1.0 - beta_two) * lowrank * lowrank
            corr_one = 1.0 - beta_one**STEP
            corr_two = 1.0 - beta_two**STEP
            result = (first_new / corr_one / (jnp.sqrt(second_new / corr_two) + adam_eps)).astype(jnp.bfloat16)
            for i in range(2):
                direction[2 * b + i] = result[:, lanes_at(i)]
            for i, (value, codes) in enumerate(((first_new, ofc_ref), (second_new, osc_ref))):
                peak = jnp.max(jnp.abs(value), axis=1, keepdims=True) + scale_eps
                codes[row, lane] = (value / peak).astype(jnp.bfloat16)
                mine_peaks[i].append(peak)
        for i in range(2):
            peaks[i].append(jnp.concatenate(mine_peaks[i], axis=1))
        for part in range(3):
            at = (mine + block_row(half, part, chip)) // PW
            for j, block in enumerate(LANES_OF[half][part]):
                whole[at + j] = direction[block]

    mine, theirs = core * HALF_ROWS, other * HALF_ROWS
    started, forwards = [], []

    def copy_of(start, size, send, recv, target):
        where = whole.at[pl.ds(start // PW, size // PW)]
        return remote(where, where, send, recv, target)

    def spread(start, size, send, recv, target):
        started.append(copy_of(mine + start, size, send, recv, target))
        started[-1].start()

    def forward(start, size):
        index = len(forwards)
        forwards.append((start, size))
        spread(start, size, fwd_send.at[index], fwd_recv.at[index], sibling)

    def landed(start, size, recv):
        copy_of(mine + start, size, first_send.at[0], recv, sibling).wait_recv()
        return start, size

    def direct_start(stage, half):
        for part in range(3):
            order, size, base = part_of(half, part)
            if stage == 2:
                piece = block_row(half, part, chip), size
            else:
                for step in range(1, RING):
                    start = block_row(half, part, shifted(chip, order[2], RING - step))
                    landed(start, size, ag_recv.at[18 + half * 9 + part * 3 + step - 1])
                piece = sub_row(half, part, chip[order[0]], chip[order[1]]), size * RING
            for step in (2, 1, 3):
                sem = (stage - 1) * 18 + half * 9 + part * 3 + step - 1
                to = device_of(shifted(chip, order[stage], step), core)
                spread(*piece, ag_send.at[sem], ag_recv.at[sem], to)

    def wide_piece(half, part, a_off, way):
        order, size, base = part_of(half, part)
        return sub_row(half, part, lax.rem(chip[order[0]] + a_off, RING), 2 * way), 2 * size * RING

    def near_start(half):
        for part in range(3):
            order, size, base = part_of(half, part)
            for step in range(1, RING):
                start = sub_row(half, part, chip[order[0]], lax.rem(chip[order[1]] + RING - step, RING))
                landed(start, size * RING, ag_recv.at[half * 9 + part * 3 + step - 1])
            for turn in range(2):
                for way, flow in enumerate((1, RING - 1)):
                    content = way ^ turn
                    sem = half * 12 + part * 4 + way * 2 + content
                    to = device_of(shifted(chip, order[0], flow), core)
                    spread(*wide_piece(half, part, 0, content), near_send.at[sem], near_recv.at[sem], to)
            forward(sub_row(half, part, chip[order[0]], 0), size * RING * RING)

    def near_landed(half, turn):
        for part in range(3):
            order = ORDERS[part]
            for way, flow in enumerate((1, RING - 1)):
                content = way ^ turn
                piece = landed(
                    *wide_piece(half, part, RING - flow, content),
                    near_recv.at[half * 12 + part * 4 + way * 2 + content],
                )
                if turn == 0:
                    sem = 24 + half * 6 + part * 2 + way
                    to = device_of(shifted(chip, order[0], flow), core)
                    spread(*piece, near_send.at[sem], near_recv.at[sem], to)
                forward(*piece)

    def far_landed(half):
        for part in range(3):
            for way in range(2):
                forward(*landed(*wide_piece(half, part, 2, way), near_recv.at[24 + half * 6 + part * 2 + way]))

    project(0)
    opening_start(0, 0)
    opening_start(1, 0)
    project(1)
    opening_start(0, 1)
    pass_on(0)
    opening_start(1, 1)
    pass_on(1)
    first_done(0)
    middle_done(0)
    first_done(1)
    adam(0)
    direct_start(2, 0)
    middle_done(1)
    direct_start(1, 0)
    adam(1)
    direct_start(2, 1)
    near_start(0)
    direct_start(1, 1)
    near_start(1)
    for turn in range(2):
        for half in range(2):
            near_landed(half, turn)
    far_landed(0)
    far_landed(1)
    ofs_ref[...] = jnp.concatenate(peaks[0], axis=0).T
    oss_ref[...] = jnp.concatenate(peaks[1], axis=0).T
    for index, (start, size) in enumerate(forwards):
        copy_of(theirs + start, size, first_send.at[0], fwd_recv.at[index], sibling).wait_recv()

    proj_copy.wait_send()
    for copy in pair:
        copy.wait_send()
    for stage in (opening, middle, closing):
        for copy in stage.values():
            copy.wait_send()
    for copy in started:
        copy.wait_send()


def finish(table_ref, whole, proj_hbm, *refs):
    passed, update_hbm, outs = refs[:4], refs[4], refs[5:9]
    proj_ref, natural, update_ref, out_sem, pass_sem, proj_sem = refs[9:]
    load = pltpu.make_async_copy(proj_hbm, proj_ref, proj_sem)
    load.start()
    passing = [pltpu.make_async_copy(passed[i], outs[i], pass_sem.at[i]) for i in range(4)]
    for copy in passing:
        copy.start()
    tile = natural.shape[0]
    steps = update_ref.shape[1] // tile
    stores = []
    for t in range(steps):
        cols = pl.ds(t * tile, tile)
        stores.append(pltpu.make_async_copy(update_ref.at[:, cols], update_hbm.at[:, cols], out_sem.at[t]))

    load.wait()

    @pl.loop(0, steps)
    def _(t):
        for p in range(tile // PW):
            packed = table_ref[t * (tile // PW) + p]
            half = lax.shift_right_logical(packed, 30)
            starts = [lax.shift_right_logical(packed, 10 * part) & 1023 for part in range(3)]
            sources = starts + [starts[0] + 1 + half * (starts[1] - starts[0])]
            for lane, source in enumerate(sources):
                natural[p * PW : (p + 1) * PW, lanes_at(lane)] = whole[source]
        product = lax.dot_general(
            proj_ref[...], natural[...], (((1,), (1,)), ((), ())), preferred_element_type=jnp.float32
        )
        cols = pl.ds(pl.multiple_of(t * tile, tile), tile)
        update_ref[:, cols] = product.astype(jnp.bfloat16)
        pltpu.make_async_copy(update_ref.at[:, cols], update_hbm.at[:, cols], out_sem.at[t]).start()

    for copy in stores + passing:
        copy.wait()


def in_hbm(array):
    return pltpu.with_memory_space_constraint(array, pltpu.HBM)


def local(gradients, projection, plan, first_codes, first_scales, second_codes, second_scales):
    panel_count = plan.shape[0]
    position = jnp.arange(panel_count, dtype=jnp.int32)
    owner = position // 2
    half = position % 2
    chip = {"x": owner // 32, "z": owner // 8 % RING, "y": owner // 2 % RING}
    base = (owner % 2) * HALF_ROWS
    starts = [
        (base + jnp.where(half == 0, block_row(0, part, chip), block_row(1, part, chip))) // PW for part in range(3)
    ]
    packed = starts[0] + starts[1] * 1024 + starts[2] * 1024 * 1024 + half * 1024 * 1024 * 1024
    found = plan[None, :] == position[:, None]
    table = jnp.sum(jnp.where(found, packed[None, :], 0), axis=1)

    bf16, f32 = jnp.bfloat16, jnp.float32
    vmem = pl.BlockSpec(memory_space=pltpu.VMEM)
    smem = pl.BlockSpec(memory_space=pltpu.SMEM)
    hbm = pl.BlockSpec(memory_space=pltpu.HBM)
    sem = pltpu.SemaphoreType.DMA
    rows_count, col_count = gradients.shape[1:]
    half_cols = col_count // 2
    whole, *moments = pl.pallas_call(
        kernel,
        out_shape=(
            pltpu.VMEM((2 * HALF_ROWS // PW, PW, LANES), bf16),
            jax.ShapeDtypeStruct(first_codes.shape, bf16),
            jax.ShapeDtypeStruct(first_scales.shape[::-1], f32),
            jax.ShapeDtypeStruct(second_codes.shape, bf16),
            jax.ShapeDtypeStruct(second_scales.shape[::-1], f32),
        ),
        in_specs=[smem] + [hbm] * 6,
        out_specs=(vmem, vmem, vmem, vmem, vmem),
        scratch_shapes=[
            pltpu.VMEM(projection.shape, bf16),
            pltpu.VMEM(first_codes.shape, bf16),
            pltpu.VMEM(first_scales.shape[::-1], f32),
            pltpu.VMEM(second_codes.shape, bf16),
            pltpu.VMEM(second_scales.shape[::-1], f32),
            pltpu.VMEM((rows_count, col_count), bf16),
            pltpu.VMEM((col_count // PW, PW, rows_count), bf16),
            pltpu.VMEM((half_cols, rows_count), bf16),
            pltpu.VMEM((half_cols, rows_count), bf16),
            pltpu.VMEM((half_cols, rows_count), bf16),
            pltpu.VMEM(projection.shape, bf16),
            pltpu.VMEM((HALF_ROWS, LANES), bf16),
            pltpu.VMEM((HALF_ROWS // 4, LANES), bf16),
            pltpu.VMEM((HALF_ROWS // 2, LANES), bf16),
            pltpu.VMEM((HALF_ROWS // 4, LANES), bf16),
            pltpu.VMEM((HALF_ROWS * 3 // 16, LANES), bf16),
            pltpu.VMEM((HALF_ROWS // 16, LANES), bf16),
            pltpu.VMEM((HALF_ROWS * 3 // 64, LANES), bf16),
            sem((4,)), sem((5,)), sem((3,)), sem((3,)), sem((36,)), sem((36,)), sem((36,)), sem((36,)), sem((36,)), sem((36,)),
            sem((36,)), sem((36,)), sem((42,)), sem((42,)),
        ],
        compiler_params=pltpu.CompilerParams(
            collective_id=0, has_side_effects=True, vmem_limit_bytes=54 * 1024 * 1024
        ),
    )(plan, *map(in_hbm, (gradients, projection, first_codes, first_scales.T, second_codes, second_scales.T)))
    update, first_out, first_peak, second_out, second_peak = pl.pallas_call(
        finish,
        out_shape=[jax.ShapeDtypeStruct((rows_count, col_count), bf16)]
        + [jax.ShapeDtypeStruct(moment.shape, moment.dtype) for moment in moments],
        in_specs=[smem, vmem] + [hbm] * 5,
        out_specs=[hbm] * 5,
        scratch_shapes=[
            pltpu.VMEM(projection.shape, bf16),
            pltpu.VMEM((512, RANK), bf16),
            pltpu.VMEM((rows_count, col_count), bf16),
            sem((col_count // 512,)),
            sem((4,)),
            sem,
        ],
        compiler_params=pltpu.CompilerParams(vmem_limit_bytes=24 * 1024 * 1024),
    )(table, pltpu.with_memory_space_constraint(whole, pltpu.VMEM), in_hbm(projection), *map(in_hbm, moments))
    return update, first_out, first_peak.T, second_out, second_peak.T


def solution(mesh):
    in_specs = (
        P("replica", "fsdp", None),
        P("fsdp", None),
        P(),
        P(("replica", "fsdp"), None),
        P(("replica", "fsdp"), None),
        P(("replica", "fsdp"), None),
        P(("replica", "fsdp"), None),
    )
    out_specs = (
        P("fsdp", None),
        P(("replica", "fsdp"), None),
        P(("replica", "fsdp"), None),
        P(("replica", "fsdp"), None),
        P(("replica", "fsdp"), None),
    )
    return jax.shard_map(local, mesh=mesh, in_specs=in_specs, out_specs=out_specs, check_vma=False)
```

```python
import functools

import jax
import jax.numpy as jnp
from jax import lax
from jax.experimental import pallas as pl
from jax.experimental.pallas import tpu as pltpu
from jax.sharding import PartitionSpec as P

PW = 32
QB = 256
STEP = 2
RING = 4
LANES = 128

beta_one = 0.9
beta_two = 0.999
adam_eps = 1e-08
scale_eps = 1e-06

MESH = pl.DeviceIdType.MESH

CHIPS = RING**3
OWNED = 64
RANK = 512
HALF_ROWS = 256 * CHIPS
ORDERS = (("x", "y", "z"), ("y", "z", "x"), ("z", "x", "y"))
LANES_OF = (((0, 3), (1,), (2,)), ((0,), (1, 3), (2,)))
BOTH = [(half, part) for half in range(2) for part in range(3)]


def part_of(half, part):
    sizes = [PW * len(lanes) for lanes in LANES_OF[half]]
    return ORDERS[part], sizes[part], half * HALF_ROWS // 2 + sum(sizes[:part]) * CHIPS


def block_row(half, part, chip):
    order, size, base = part_of(half, part)
    a, b, c = (chip[name] for name in order)
    return base + ((a * RING + b) * RING + c) * size


def shifted(chip, axis, step):
    moved = dict(chip)
    moved[axis] = lax.rem(chip[axis] + step, RING)
    return moved


def device_of(chip, core):
    return (chip["x"], (chip["z"] * RING + chip["y"]) * 2 + core)


def rows(start, size):
    return pl.ds(pl.multiple_of(start, 32), size)


def lanes_at(block):
    return slice(block * LANES, (block + 1) * LANES)


def kernel(
    plan_ref, grad_hbm, proj_hbm, fc_hbm, fs_hbm, sc_hbm, ss_hbm,
    whole, ofc_ref, ofs_ref, osc_ref, oss_ref,
    proj_ref, fc_ref, fs_ref, sc_ref, ss_ref, grad_ref, turned, other_out, other_in, own_rows, proj_other,
    sums1, transit, recv1, sums2, recv2, sums3, recv3,
    grad_sem, small_sem, pair_send, pair_recv, first_send, first_recv, rs_send, rs_recv, near_send, near_recv, ag_send, ag_recv, fwd_send, fwd_recv,
):
    replica = lax.axis_index("replica")
    inner = lax.axis_index("fsdp")
    chip = {"x": replica, "z": inner // 8, "y": lax.rem(inner // 2, RING)}
    core = lax.rem(inner, 2)
    other = 1 - core
    sibling = device_of(chip, other)
    cols = grad_hbm.shape[2] // RING

    loads = []
    for j in range(RING):
        loads.append(
            pltpu.make_async_copy(
                grad_hbm.at[0, :, pl.ds(j * cols, cols)], grad_ref.at[:, pl.ds(j * cols, cols)], grad_sem.at[j]
            )
        )
        loads[-1].start()

    small = []
    for i, (source, target) in enumerate(
        ((proj_hbm, proj_ref), (fc_hbm, fc_ref), (fs_hbm, fs_ref), (sc_hbm, sc_ref), (ss_hbm, ss_ref))
    ):
        small.append(pltpu.make_async_copy(source, target, small_sem.at[i]))
        small[-1].start()

    barrier = pltpu.get_barrier_semaphore()
    pl.semaphore_signal(barrier, inc=1, device_id=sibling, device_id_type=MESH)
    for axis in ("x", "y", "z"):
        for step in range(1, RING):
            pl.semaphore_signal(
                barrier, inc=1, device_id=device_of(shifted(chip, axis, step), core), device_id_type=MESH
            )

    for j in range(RING):
        loads[j].wait()

        @pl.loop(0, cols // 256)
        def _(t, j=j):
            at = pl.multiple_of(j * cols + t * 256, 256)
            block = grad_ref[:, pl.ds(at, 256)].T
            turned[pl.ds(at // PW, 256 // PW)] = block.reshape(256 // PW, PW, block.shape[1])

    for copy in small:
        copy.wait()
    pl.semaphore_wait(barrier, 3 * (RING - 1) + 1)

    def remote(src, dst, send, recv, target):
        return pltpu.make_async_remote_copy(
            src_ref=src, dst_ref=dst, send_sem=send, recv_sem=recv, device_id=target, device_id_type=MESH
        )

    proj_copy = remote(proj_ref, proj_other, pair_send.at[2], pair_recv.at[2], sibling)
    proj_copy.start()

    span = CHIPS * PW

    def pick(target, which, half):
        @pl.loop(0, CHIPS)
        def _(t):
            target[rows(half * span + t * PW, PW), :] = turned[plan_ref[(t * 2 + which) * 2 + half]]

    pair = []
    for half in range(2):
        pick(other_out, other, half)
        part_rows = pl.ds(half * span, span)
        pair.append(
            remote(
                other_out.at[part_rows, :], other_in.at[part_rows, :],
                pair_send.at[half], pair_recv.at[half], sibling,
            )
        )
        pair[-1].start()

    def project(half):
        pick(own_rows, core, half)
        if half == 0:
            proj_copy.wait_recv()
        pair[half].wait_recv()

        @pl.loop(0, CHIPS // 8)
        def _(t):
            at = rows(half * span + t * 8 * PW, 8 * PW)
            product = jnp.dot(own_rows[at, :], proj_ref[...], preferred_element_type=jnp.float32)
            product += jnp.dot(other_in[at, :], proj_other[...], preferred_element_type=jnp.float32)
            for i in range(8):
                to = {"x": t // 2, "z": (t % 2) * 2 + i // 4, "y": i % 4}
                for part in range(3):
                    for j, block in enumerate(LANES_OF[half][part]):
                        sums1[rows(block_row(half, part, to) + j * PW, PW), :] = product[
                            i * PW : (i + 1) * PW, lanes_at(block)
                        ].astype(jnp.bfloat16)

    def sub_row(half, part, a, b):
        order = ORDERS[part]
        return block_row(half, part, {order[0]: a, order[1]: b, order[2]: 0})

    opening, middle, closing = {}, {}, {}
    for half, part in BOTH:
        order, size, base = part_of(half, part)
        a = chip[order[0]]
        message = 2 * size * RING
        for way, flow in enumerate((1, RING - 1)):
            onward = device_of(shifted(chip, order[0], flow), core)
            backward = device_of(shifted(chip, order[0], RING - flow), core)
            sem = half * 6 + part * 2 + way
            land = base // 2 + way * 2 * message
            for kind, (steps, landing, place, target) in enumerate(
                (
                    (2, transit, base // 4 + way * message, onward),
                    (RING - flow, recv1, land, backward),
                    (flow, recv1, land + message, onward),
                )
            ):
                opening[kind, half, part, way] = remote(
                    sums1.at[rows(sub_row(half, part, lax.rem(a + steps, RING), 2 * way), message), :],
                    landing.at[pl.ds(place, message), :],
                    first_send.at[12 * kind + sem], first_recv.at[12 * kind + sem], target,
                )
        for stage, source, landing, copies in ((1, sums2, recv2, middle), (2, sums3, recv3, closing)):
            unit = size * RING ** (2 - stage)
            origin = base // RING**stage
            for step in range(1, RING):
                to = shifted(chip, order[stage], step)
                sem = (stage - 1) * 18 + half * 9 + part * 3 + step - 1
                copies[half, part, step] = remote(
                    source.at[rows(origin + to[order[stage]] * unit, unit), :],
                    landing.at[pl.ds(3 * base // RING ** (stage + 1) + (step - 1) * unit, unit), :],
                    rs_send.at[sem], rs_recv.at[sem], device_of(to, core),
                )

    def opening_start(kind, half):
        for part in range(3):
            for way in range(2):
                opening[kind, half, part, way].start()

    def add(count, target, at, *terms):
        tile = 128

        @pl.loop(0, count // tile)
        def _(t):
            total = sum(ref[rows(row + t * tile, tile), :].astype(jnp.float32) for ref, row in terms)
            target[rows(at + t * tile, tile), :] = total.astype(jnp.bfloat16)

    def pass_on(half):
        for part in range(3):
            order, size, base = part_of(half, part)
            message = 2 * size * RING
            for way, flow in enumerate((1, RING - 1)):
                opening[0, half, part, way].wait_recv()
                own = sub_row(half, part, lax.rem(chip[order[0]] + flow, RING), 2 * way)
                add(message, sums1, own, (sums1, own), (transit, base // 4 + way * message))
                opening[2, half, part, way].start()

    def first_done(half):
        for part in range(3):
            order, size, base = part_of(half, part)
            message = 2 * size * RING
            for way in range(2):
                opening[1, half, part, way].wait_recv()
                opening[2, half, part, way].wait_recv()
                own = sub_row(half, part, chip[order[0]], 2 * way)
                land = base // 2 + way * 2 * message
                add(
                    message, sums2, base // RING + way * message,
                    (sums1, own), (recv1, land), (recv1, land + message),
                )
            for step in (2, 1, 3):
                middle[half, part, step].start()

    def middle_done(half):
        for part in range(3):
            order, size, base = part_of(half, part)
            for step in range(1, RING):
                middle[half, part, step].wait_recv()
            unit = size * RING
            own = base // RING + chip[order[1]] * unit
            landings = [(recv2, 3 * base // RING**2 + i * unit) for i in range(3)]
            add(unit, sums3, base // RING**2, (sums2, own), *landings)
            for step in (2, 1, 3):
                closing[half, part, step].start()

    first_scales, second_scales = fs_ref[...].T, ss_ref[...].T
    peaks = ([], [])

    def adam(half):
        low = {}
        for part in range(3):
            order, size, base = part_of(half, part)
            for step in range(1, RING):
                closing[half, part, step].wait_recv()
            total = sums3[rows(base // 16 + chip[order[2]] * size, size), :].astype(jnp.float32)
            for i in range(3):
                total += recv3[pl.ds(3 * base // 64 + i * size, size), :].astype(jnp.float32)
            for j, block in enumerate(LANES_OF[half][part]):
                low[block] = total[j * PW : (j + 1) * PW, :]
        row = slice(half * PW, (half + 1) * PW)
        mine_peaks = ([], [])
        direction = {}
        for b in range(RANK // QB):
            lane = slice(b * QB, (b + 1) * QB)
            lowrank = jnp.concatenate([low[2 * b], low[2 * b + 1]], axis=1)
            first = fc_ref[row, lane].astype(jnp.float32) * first_scales[row, b : b + 1]
            second = sc_ref[row, lane].astype(jnp.float32) * second_scales[row, b : b + 1]
            first_new = beta_one * first + (1.0 - beta_one) * lowrank
            second_new = beta_two * second + (1.0 - beta_two) * lowrank * lowrank
            corr_one = 1.0 - beta_one**STEP
            corr_two = 1.0 - beta_two**STEP
            result = (first_new / corr_one / (jnp.sqrt(second_new / corr_two) + adam_eps)).astype(jnp.bfloat16)
            for i in range(2):
                direction[2 * b + i] = result[:, lanes_at(i)]
            for i, (value, codes) in enumerate(((first_new, ofc_ref), (second_new, osc_ref))):
                peak = jnp.max(jnp.abs(value), axis=1, keepdims=True) + scale_eps
                codes[row, lane] = (value / peak).astype(jnp.bfloat16)
                mine_peaks[i].append(peak)
        for i in range(2):
            peaks[i].append(jnp.concatenate(mine_peaks[i], axis=1))
        for part in range(3):
            at = (mine + block_row(half, part, chip)) // PW
            for j, block in enumerate(LANES_OF[half][part]):
                whole[at + j] = direction[block]

    mine, theirs = core * HALF_ROWS, other * HALF_ROWS
    started, forwards = [], []

    def copy_of(start, size, send, recv, target):
        where = whole.at[pl.ds(start // PW, size // PW)]
        return remote(where, where, send, recv, target)

    def spread(start, size, send, recv, target):
        started.append(copy_of(mine + start, size, send, recv, target))
        started[-1].start()

    def forward(start, size):
        index = len(forwards)
        forwards.append((start, size))
        spread(start, size, fwd_send.at[index], fwd_recv.at[index], sibling)

    def landed(start, size, recv):
        copy_of(mine + start, size, first_send.at[0], recv, sibling).wait_recv()
        return start, size

    def direct_start(stage, half):
        for part in range(3):
            order, size, base = part_of(half, part)
            if stage == 2:
                piece = block_row(half, part, chip), size
            else:
                for step in range(1, RING):
                    start = block_row(half, part, shifted(chip, order[2], RING - step))
                    landed(start, size, ag_recv.at[18 + half * 9 + part * 3 + step - 1])
                piece = sub_row(half, part, chip[order[0]], chip[order[1]]), size * RING
            for step in (2, 1, 3):
                sem = (stage - 1) * 18 + half * 9 + part * 3 + step - 1
                to = device_of(shifted(chip, order[stage], step), core)
                spread(*piece, ag_send.at[sem], ag_recv.at[sem], to)

    def wide_piece(half, part, a_off, way):
        order, size, base = part_of(half, part)
        return sub_row(half, part, lax.rem(chip[order[0]] + a_off, RING), 2 * way), 2 * size * RING

    def near_start(half):
        for part in range(3):
            order, size, base = part_of(half, part)
            for step in range(1, RING):
                start = sub_row(half, part, chip[order[0]], lax.rem(chip[order[1]] + RING - step, RING))
                landed(start, size * RING, ag_recv.at[half * 9 + part * 3 + step - 1])
            for turn in range(2):
                for way, flow in enumerate((1, RING - 1)):
                    content = way ^ turn
                    sem = half * 12 + part * 4 + way * 2 + content
                    to = device_of(shifted(chip, order[0], flow), core)
                    spread(*wide_piece(half, part, 0, content), near_send.at[sem], near_recv.at[sem], to)
            forward(sub_row(half, part, chip[order[0]], 0), size * RING * RING)

    def near_landed(half, turn):
        for part in range(3):
            order = ORDERS[part]
            for way, flow in enumerate((1, RING - 1)):
                content = way ^ turn
                piece = landed(
                    *wide_piece(half, part, RING - flow, content),
                    near_recv.at[half * 12 + part * 4 + way * 2 + content],
                )
                if turn == 0:
                    sem = 24 + half * 6 + part * 2 + way
                    to = device_of(shifted(chip, order[0], flow), core)
                    spread(*piece, near_send.at[sem], near_recv.at[sem], to)
                forward(*piece)

    def far_landed(half):
        for part in range(3):
            for way in range(2):
                forward(*landed(*wide_piece(half, part, 2, way), near_recv.at[24 + half * 6 + part * 2 + way]))

    project(0)
    opening_start(0, 0)
    opening_start(1, 0)
    project(1)
    opening_start(0, 1)
    pass_on(0)
    opening_start(1, 1)
    pass_on(1)
    first_done(0)
    middle_done(0)
    first_done(1)
    adam(0)
    direct_start(2, 0)
    middle_done(1)
    direct_start(1, 0)
    adam(1)
    direct_start(2, 1)
    near_start(0)
    direct_start(1, 1)
    near_start(1)
    for turn in range(2):
        for half in range(2):
            near_landed(half, turn)
    far_landed(0)
    far_landed(1)
    ofs_ref[...] = jnp.concatenate(peaks[0], axis=0).T
    oss_ref[...] = jnp.concatenate(peaks[1], axis=0).T
    for index, (start, size) in enumerate(forwards):
        copy_of(theirs + start, size, first_send.at[0], fwd_recv.at[index], sibling).wait_recv()

    proj_copy.wait_send()
    for copy in pair:
        copy.wait_send()
    for stage in (opening, middle, closing):
        for copy in stage.values():
            copy.wait_send()
    for copy in started:
        copy.wait_send()


def finish(table_ref, whole, proj_hbm, *refs):
    passed, update_hbm, outs = refs[:4], refs[4], refs[5:9]
    proj_ref, natural, update_ref, out_sem, pass_sem, proj_sem = refs[9:]
    load = pltpu.make_async_copy(proj_hbm, proj_ref, proj_sem)
    load.start()
    passing = [pltpu.make_async_copy(passed[i], outs[i], pass_sem.at[i]) for i in range(4)]
    for copy in passing:
        copy.start()
    tile = natural.shape[0]
    steps = update_ref.shape[1] // tile
    stores = []
    for t in range(steps):
        cols = pl.ds(t * tile, tile)
        stores.append(pltpu.make_async_copy(update_ref.at[:, cols], update_hbm.at[:, cols], out_sem.at[t]))

    load.wait()

    @pl.loop(0, steps)
    def _(t):
        pieces = []
        for p in range(tile // PW):
            packed = table_ref[t * (tile // PW) + p]
            half = lax.shift_right_logical(packed, 30)
            starts = [lax.shift_right_logical(packed, 10 * part) & 1023 for part in range(3)]
            sources = starts + [starts[0] + 1 + half * (starts[1] - starts[0])]
            pieces.append(jnp.concatenate([whole[source] for source in sources], axis=1))
        picked = jnp.concatenate(pieces, axis=0)
        product = lax.dot_general(
            proj_ref[...], picked, (((1,), (1,)), ((), ())), preferred_element_type=jnp.float32
        )
        cols = pl.ds(pl.multiple_of(t * tile, tile), tile)
        update_ref[:, cols] = product.astype(jnp.bfloat16)
        pltpu.make_async_copy(update_ref.at[:, cols], update_hbm.at[:, cols], out_sem.at[t]).start()

    for copy in stores + passing:
        copy.wait()


def in_hbm(array):
    return pltpu.with_memory_space_constraint(array, pltpu.HBM)


def local(gradients, projection, plan, first_codes, first_scales, second_codes, second_scales):
    panel_count = plan.shape[0]
    position = jnp.arange(panel_count, dtype=jnp.int32)
    owner = position // 2
    half = position % 2
    chip = {"x": owner // 32, "z": owner // 8 % RING, "y": owner // 2 % RING}
    base = (owner % 2) * HALF_ROWS
    starts = [
        (base + jnp.where(half == 0, block_row(0, part, chip), block_row(1, part, chip))) // PW for part in range(3)
    ]
    packed = starts[0] + starts[1] * 1024 + starts[2] * 1024 * 1024 + half * 1024 * 1024 * 1024
    found = plan[None, :] == position[:, None]
    table = jnp.sum(jnp.where(found, packed[None, :], 0), axis=1)

    bf16, f32 = jnp.bfloat16, jnp.float32
    vmem = pl.BlockSpec(memory_space=pltpu.VMEM)
    smem = pl.BlockSpec(memory_space=pltpu.SMEM)
    hbm = pl.BlockSpec(memory_space=pltpu.HBM)
    sem = pltpu.SemaphoreType.DMA
    rows_count, col_count = gradients.shape[1:]
    half_cols = col_count // 2
    whole, *moments = pl.pallas_call(
        kernel,
        out_shape=(
            pltpu.VMEM((2 * HALF_ROWS // PW, PW, LANES), bf16),
            jax.ShapeDtypeStruct(first_codes.shape, bf16),
            jax.ShapeDtypeStruct(first_scales.shape[::-1], f32),
            jax.ShapeDtypeStruct(second_codes.shape, bf16),
            jax.ShapeDtypeStruct(second_scales.shape[::-1], f32),
        ),
        in_specs=[smem] + [hbm] * 6,
        out_specs=(vmem, vmem, vmem, vmem, vmem),
        scratch_shapes=[
            pltpu.VMEM(projection.shape, bf16),
            pltpu.VMEM(first_codes.shape, bf16),
            pltpu.VMEM(first_scales.shape[::-1], f32),
            pltpu.VMEM(second_codes.shape, bf16),
            pltpu.VMEM(second_scales.shape[::-1], f32),
            pltpu.VMEM((rows_count, col_count), bf16),
            pltpu.VMEM((col_count // PW, PW, rows_count), bf16),
            pltpu.VMEM((half_cols, rows_count), bf16),
            pltpu.VMEM((half_cols, rows_count), bf16),
            pltpu.VMEM((half_cols, rows_count), bf16),
            pltpu.VMEM(projection.shape, bf16),
            pltpu.VMEM((HALF_ROWS, LANES), bf16),
            pltpu.VMEM((HALF_ROWS // 4, LANES), bf16),
            pltpu.VMEM((HALF_ROWS // 2, LANES), bf16),
            pltpu.VMEM((HALF_ROWS // 4, LANES), bf16),
            pltpu.VMEM((HALF_ROWS * 3 // 16, LANES), bf16),
            pltpu.VMEM((HALF_ROWS // 16, LANES), bf16),
            pltpu.VMEM((HALF_ROWS * 3 // 64, LANES), bf16),
            sem((4,)), sem((5,)), sem((3,)), sem((3,)), sem((36,)), sem((36,)), sem((36,)), sem((36,)), sem((36,)), sem((36,)),
            sem((36,)), sem((36,)), sem((42,)), sem((42,)),
        ],
        compiler_params=pltpu.CompilerParams(
            collective_id=0, has_side_effects=True, vmem_limit_bytes=54 * 1024 * 1024
        ),
    )(plan, *map(in_hbm, (gradients, projection, first_codes, first_scales.T, second_codes, second_scales.T)))
    update, first_out, first_peak, second_out, second_peak = pl.pallas_call(
        finish,
        out_shape=[jax.ShapeDtypeStruct((rows_count, col_count), bf16)]
        + [jax.ShapeDtypeStruct(moment.shape, moment.dtype) for moment in moments],
        in_specs=[smem, vmem] + [hbm] * 5,
        out_specs=[hbm] * 5,
        scratch_shapes=[
            pltpu.VMEM(projection.shape, bf16),
            pltpu.VMEM((2048, RANK), bf16),
            pltpu.VMEM((rows_count, col_count), bf16),
            sem((col_count // 2048,)),
            sem((4,)),
            sem,
        ],
        compiler_params=pltpu.CompilerParams(vmem_limit_bytes=24 * 1024 * 1024),
    )(table, pltpu.with_memory_space_constraint(whole, pltpu.VMEM), in_hbm(projection), *map(in_hbm, moments))
    return update, first_out, first_peak.T, second_out, second_peak.T


def solution(mesh):
    in_specs = (
        P("replica", "fsdp", None),
        P("fsdp", None),
        P(),
        P(("replica", "fsdp"), None),
        P(("replica", "fsdp"), None),
        P(("replica", "fsdp"), None),
        P(("replica", "fsdp"), None),
    )
    out_specs = (
        P("fsdp", None),
        P(("replica", "fsdp"), None),
        P(("replica", "fsdp"), None),
        P(("replica", "fsdp"), None),
        P(("replica", "fsdp"), None),
    )
    return jax.shard_map(local, mesh=mesh, in_specs=in_specs, out_specs=out_specs, check_vma=False)
```

```python
import functools

import jax
import jax.numpy as jnp
from jax import lax
from jax.experimental import pallas as pl
from jax.experimental.pallas import tpu as pltpu
from jax.sharding import PartitionSpec as P

PW = 32
QB = 256
STEP = 2
RING = 4
LANES = 128

beta_one = 0.9
beta_two = 0.999
adam_eps = 1e-08
scale_eps = 1e-06

MESH = pl.DeviceIdType.MESH

CHIPS = RING**3
OWNED = 64
RANK = 512
HALF_ROWS = 256 * CHIPS
ORDERS = (("x", "y", "z"), ("y", "z", "x"), ("z", "x", "y"))
LANES_OF = (((0, 3), (1,), (2,)), ((0,), (1, 3), (2,)))
BOTH = [(half, part) for half in range(2) for part in range(3)]


def part_of(half, part):
    sizes = [PW * len(lanes) for lanes in LANES_OF[half]]
    return ORDERS[part], sizes[part], half * HALF_ROWS // 2 + sum(sizes[:part]) * CHIPS


def block_row(half, part, chip):
    order, size, base = part_of(half, part)
    a, b, c = (chip[name] for name in order)
    return base + ((a * RING + b) * RING + c) * size


def shifted(chip, axis, step):
    moved = dict(chip)
    moved[axis] = lax.rem(chip[axis] + step, RING)
    return moved


def device_of(chip, core):
    return (chip["x"], (chip["z"] * RING + chip["y"]) * 2 + core)


def rows(start, size):
    return pl.ds(pl.multiple_of(start, 32), size)


def lanes_at(block):
    return slice(block * LANES, (block + 1) * LANES)


def kernel(
    plan_ref, grad_hbm, proj_hbm, fc_hbm, fs_hbm, sc_hbm, ss_hbm,
    whole, ofc_ref, ofs_ref, osc_ref, oss_ref,
    proj_ref, fc_ref, fs_ref, sc_ref, ss_ref, grad_ref, turned, other_out, other_in, own_rows, proj_other,
    sums1, transit, recv1, sums2, recv2, sums3, recv3,
    grad_sem, small_sem, pair_send, pair_recv, first_send, first_recv, rs_send, rs_recv, near_send, near_recv, ag_send, ag_recv, fwd_send, fwd_recv,
):
    replica = lax.axis_index("replica")
    inner = lax.axis_index("fsdp")
    chip = {"x": replica, "z": inner // 8, "y": lax.rem(inner // 2, RING)}
    core = lax.rem(inner, 2)
    other = 1 - core
    sibling = device_of(chip, other)
    cols = grad_hbm.shape[2] // RING

    loads = []
    for j in range(RING):
        loads.append(
            pltpu.make_async_copy(
                grad_hbm.at[0, :, pl.ds(j * cols, cols)], grad_ref.at[:, pl.ds(j * cols, cols)], grad_sem.at[j]
            )
        )
        loads[-1].start()

    small = []
    for i, (source, target) in enumerate(
        ((proj_hbm, proj_ref), (fc_hbm, fc_ref), (fs_hbm, fs_ref), (sc_hbm, sc_ref), (ss_hbm, ss_ref))
    ):
        small.append(pltpu.make_async_copy(source, target, small_sem.at[i]))
        small[-1].start()

    barrier = pltpu.get_barrier_semaphore()
    pl.semaphore_signal(barrier, inc=1, device_id=sibling, device_id_type=MESH)
    for axis in ("x", "y", "z"):
        for step in range(1, RING):
            pl.semaphore_signal(
                barrier, inc=1, device_id=device_of(shifted(chip, axis, step), core), device_id_type=MESH
            )

    for j in range(RING):
        loads[j].wait()

        @pl.loop(0, cols // 256)
        def _(t, j=j):
            at = pl.multiple_of(j * cols + t * 256, 256)
            block = grad_ref[:, pl.ds(at, 256)].T
            turned[pl.ds(at // PW, 256 // PW)] = block.reshape(256 // PW, PW, block.shape[1])

    for copy in small:
        copy.wait()
    pl.semaphore_wait(barrier, 3 * (RING - 1) + 1)

    def remote(src, dst, send, recv, target):
        return pltpu.make_async_remote_copy(
            src_ref=src, dst_ref=dst, send_sem=send, recv_sem=recv, device_id=target, device_id_type=MESH
        )

    proj_copy = remote(proj_ref, proj_other, pair_send.at[2], pair_recv.at[2], sibling)
    proj_copy.start()

    span = CHIPS * PW

    def pick(target, which, half):
        @pl.loop(0, CHIPS)
        def _(t):
            target[rows(half * span + t * PW, PW), :] = turned[plan_ref[(t * 2 + which) * 2 + half]]

    pair = []
    for half in range(2):
        pick(other_out, other, half)
        part_rows = pl.ds(half * span, span)
        pair.append(
            remote(
                other_out.at[part_rows, :], other_in.at[part_rows, :],
                pair_send.at[half], pair_recv.at[half], sibling,
            )
        )
        pair[-1].start()

    def project(half):
        pick(own_rows, core, half)
        if half == 0:
            proj_copy.wait_recv()
        pair[half].wait_recv()

        @pl.loop(0, CHIPS // 8)
        def _(t):
            at = rows(half * span + t * 8 * PW, 8 * PW)
            product = jnp.dot(own_rows[at, :], proj_ref[...], preferred_element_type=jnp.float32)
            product += jnp.dot(other_in[at, :], proj_other[...], preferred_element_type=jnp.float32)
            for i in range(8):
                to = {"x": t // 2, "z": (t % 2) * 2 + i // 4, "y": i % 4}
                for part in range(3):
                    for j, block in enumerate(LANES_OF[half][part]):
                        sums1[rows(block_row(half, part, to) + j * PW, PW), :] = product[
                            i * PW : (i + 1) * PW, lanes_at(block)
                        ].astype(jnp.bfloat16)

    def sub_row(half, part, a, b):
        order = ORDERS[part]
        return block_row(half, part, {order[0]: a, order[1]: b, order[2]: 0})

    opening, middle, closing = {}, {}, {}
    for half, part in BOTH:
        order, size, base = part_of(half, part)
        a = chip[order[0]]
        message = 2 * size * RING
        for way, flow in enumerate((1, RING - 1)):
            onward = device_of(shifted(chip, order[0], flow), core)
            backward = device_of(shifted(chip, order[0], RING - flow), core)
            sem = half * 6 + part * 2 + way
            land = base // 2 + way * 2 * message
            for kind, (steps, landing, place, target) in enumerate(
                (
                    (2, transit, base // 4 + way * message, onward),
                    (RING - flow, recv1, land, backward),
                    (flow, recv1, land + message, onward),
                )
            ):
                opening[kind, half, part, way] = remote(
                    sums1.at[rows(sub_row(half, part, lax.rem(a + steps, RING), 2 * way), message), :],
                    landing.at[pl.ds(place, message), :],
                    first_send.at[12 * kind + sem], first_recv.at[12 * kind + sem], target,
                )
        for stage, source, landing, copies in ((1, sums2, recv2, middle), (2, sums3, recv3, closing)):
            unit = size * RING ** (2 - stage)
            origin = base // RING**stage
            for step in range(1, RING):
                to = shifted(chip, order[stage], step)
                sem = (stage - 1) * 18 + half * 9 + part * 3 + step - 1
                copies[half, part, step] = remote(
                    source.at[rows(origin + to[order[stage]] * unit, unit), :],
                    landing.at[pl.ds(3 * base // RING ** (stage + 1) + (step - 1) * unit, unit), :],
                    rs_send.at[sem], rs_recv.at[sem], device_of(to, core),
                )

    def opening_start(kind, half):
        for part in range(3):
            for way in range(2):
                opening[kind, half, part, way].start()

    def add(count, target, at, *terms):
        tile = 128

        @pl.loop(0, count // tile)
        def _(t):
            total = sum(ref[rows(row + t * tile, tile), :].astype(jnp.float32) for ref, row in terms)
            target[rows(at + t * tile, tile), :] = total.astype(jnp.bfloat16)

    def pass_on(half):
        for part in range(3):
            order, size, base = part_of(half, part)
            message = 2 * size * RING
            for way, flow in enumerate((1, RING - 1)):
                opening[0, half, part, way].wait_recv()
                own = sub_row(half, part, lax.rem(chip[order[0]] + flow, RING), 2 * way)
                add(message, sums1, own, (sums1, own), (transit, base // 4 + way * message))
                opening[2, half, part, way].start()

    def first_done(half):
        for part in range(3):
            order, size, base = part_of(half, part)
            message = 2 * size * RING
            for way in range(2):
                opening[1, half, part, way].wait_recv()
                opening[2, half, part, way].wait_recv()
                own = sub_row(half, part, chip[order[0]], 2 * way)
                land = base // 2 + way * 2 * message
                add(
                    message, sums2, base // RING + way * message,
                    (sums1, own), (recv1, land), (recv1, land + message),
                )
            for step in (2, 1, 3):
                middle[half, part, step].start()

    def middle_done(half):
        for part in range(3):
            order, size, base = part_of(half, part)
            for step in range(1, RING):
                middle[half, part, step].wait_recv()
            unit = size * RING
            own = base // RING + chip[order[1]] * unit
            landings = [(recv2, 3 * base // RING**2 + i * unit) for i in range(3)]
            add(unit, sums3, base // RING**2, (sums2, own), *landings)
            for step in (2, 1, 3):
                closing[half, part, step].start()

    first_scales, second_scales = fs_ref[...].T, ss_ref[...].T
    peaks = ([], [])

    def adam(half):
        low = {}
        for part in range(3):
            order, size, base = part_of(half, part)
            for step in range(1, RING):
                closing[half, part, step].wait_recv()
            total = sums3[rows(base // 16 + chip[order[2]] * size, size), :].astype(jnp.float32)
            for i in range(3):
                total += recv3[pl.ds(3 * base // 64 + i * size, size), :].astype(jnp.float32)
            for j, block in enumerate(LANES_OF[half][part]):
                low[block] = total[j * PW : (j + 1) * PW, :]
        row = slice(half * PW, (half + 1) * PW)
        mine_peaks = ([], [])
        direction = {}
        for b in range(RANK // QB):
            lane = slice(b * QB, (b + 1) * QB)
            lowrank = jnp.concatenate([low[2 * b], low[2 * b + 1]], axis=1)
            first = fc_ref[row, lane].astype(jnp.float32) * first_scales[row, b : b + 1]
            second = sc_ref[row, lane].astype(jnp.float32) * second_scales[row, b : b + 1]
            first_new = beta_one * first + (1.0 - beta_one) * lowrank
            second_new = beta_two * second + (1.0 - beta_two) * lowrank * lowrank
            corr_one = 1.0 - beta_one**STEP
            corr_two = 1.0 - beta_two**STEP
            result = (first_new / corr_one / (jnp.sqrt(second_new / corr_two) + adam_eps)).astype(jnp.bfloat16)
            for i in range(2):
                direction[2 * b + i] = result[:, lanes_at(i)]
            for i, (value, codes) in enumerate(((first_new, ofc_ref), (second_new, osc_ref))):
                peak = jnp.max(jnp.abs(value), axis=1, keepdims=True) + scale_eps
                codes[row, lane] = (value / peak).astype(jnp.bfloat16)
                mine_peaks[i].append(peak)
        for i in range(2):
            peaks[i].append(jnp.concatenate(mine_peaks[i], axis=1))
        for part in range(3):
            at = (mine + block_row(half, part, chip)) // PW
            for j, block in enumerate(LANES_OF[half][part]):
                whole[at + j] = direction[block]

    mine, theirs = core * HALF_ROWS, other * HALF_ROWS
    started, forwards = [], []

    def copy_of(start, size, send, recv, target):
        where = whole.at[pl.ds(start // PW, size // PW)]
        return remote(where, where, send, recv, target)

    def spread(start, size, send, recv, target):
        started.append(copy_of(mine + start, size, send, recv, target))
        started[-1].start()

    def forward(start, size):
        index = len(forwards)
        forwards.append((start, size))
        spread(start, size, fwd_send.at[index], fwd_recv.at[index], sibling)

    def landed(start, size, recv):
        copy_of(mine + start, size, first_send.at[0], recv, sibling).wait_recv()
        return start, size

    def direct_start(stage, half):
        for part in range(3):
            order, size, base = part_of(half, part)
            if stage == 2:
                piece = block_row(half, part, chip), size
            else:
                for step in range(1, RING):
                    start = block_row(half, part, shifted(chip, order[2], RING - step))
                    landed(start, size, ag_recv.at[18 + half * 9 + part * 3 + step - 1])
                piece = sub_row(half, part, chip[order[0]], chip[order[1]]), size * RING
            for step in (2, 1, 3):
                sem = (stage - 1) * 18 + half * 9 + part * 3 + step - 1
                to = device_of(shifted(chip, order[stage], step), core)
                spread(*piece, ag_send.at[sem], ag_recv.at[sem], to)

    def wide_piece(half, part, a_off, way):
        order, size, base = part_of(half, part)
        return sub_row(half, part, lax.rem(chip[order[0]] + a_off, RING), 2 * way), 2 * size * RING

    def near_start(half):
        for part in range(3):
            order, size, base = part_of(half, part)
            for step in range(1, RING):
                start = sub_row(half, part, chip[order[0]], lax.rem(chip[order[1]] + RING - step, RING))
                landed(start, size * RING, ag_recv.at[half * 9 + part * 3 + step - 1])
            for turn in range(2):
                for way, flow in enumerate((1, RING - 1)):
                    content = way ^ turn
                    sem = half * 12 + part * 4 + way * 2 + content
                    to = device_of(shifted(chip, order[0], flow), core)
                    spread(*wide_piece(half, part, 0, content), near_send.at[sem], near_recv.at[sem], to)
            forward(sub_row(half, part, chip[order[0]], 0), size * RING * RING)

    def near_landed(half, turn):
        for part in range(3):
            order = ORDERS[part]
            for way, flow in enumerate((1, RING - 1)):
                content = way ^ turn
                piece = landed(
                    *wide_piece(half, part, RING - flow, content),
                    near_recv.at[half * 12 + part * 4 + way * 2 + content],
                )
                if turn == 0:
                    sem = 24 + half * 6 + part * 2 + way
                    to = device_of(shifted(chip, order[0], flow), core)
                    spread(*piece, near_send.at[sem], near_recv.at[sem], to)
                forward(*piece)

    def far_landed(half):
        for part in range(3):
            for way in range(2):
                forward(*landed(*wide_piece(half, part, 2, way), near_recv.at[24 + half * 6 + part * 2 + way]))

    project(0)
    opening_start(0, 0)
    opening_start(1, 0)
    project(1)
    opening_start(0, 1)
    pass_on(0)
    opening_start(1, 1)
    pass_on(1)
    first_done(0)
    first_done(1)
    middle_done(0)
    adam(0)
    direct_start(2, 0)
    middle_done(1)
    direct_start(1, 0)
    adam(1)
    direct_start(2, 1)
    near_start(0)
    direct_start(1, 1)
    near_start(1)
    for turn in range(2):
        for half in range(2):
            near_landed(half, turn)
    far_landed(0)
    far_landed(1)
    ofs_ref[...] = jnp.concatenate(peaks[0], axis=0).T
    oss_ref[...] = jnp.concatenate(peaks[1], axis=0).T
    for index, (start, size) in enumerate(forwards):
        copy_of(theirs + start, size, first_send.at[0], fwd_recv.at[index], sibling).wait_recv()

    proj_copy.wait_send()
    for copy in pair:
        copy.wait_send()
    for stage in (opening, middle, closing):
        for copy in stage.values():
            copy.wait_send()
    for copy in started:
        copy.wait_send()


def finish(table_ref, whole, proj_hbm, *refs):
    passed, update_hbm, outs = refs[:4], refs[4], refs[5:9]
    proj_ref, natural, update_ref, out_sem, pass_sem, proj_sem = refs[9:]
    load = pltpu.make_async_copy(proj_hbm, proj_ref, proj_sem)
    load.start()
    passing = [pltpu.make_async_copy(passed[i], outs[i], pass_sem.at[i]) for i in range(4)]
    for copy in passing:
        copy.start()
    tile = natural.shape[0]
    steps = update_ref.shape[1] // tile
    stores = []
    for t in range(steps):
        cols = pl.ds(t * tile, tile)
        stores.append(pltpu.make_async_copy(update_ref.at[:, cols], update_hbm.at[:, cols], out_sem.at[t]))

    load.wait()

    @pl.loop(0, steps)
    def _(t):
        pieces = []
        for p in range(tile // PW):
            packed = table_ref[t * (tile // PW) + p]
            half = lax.shift_right_logical(packed, 30)
            starts = [lax.shift_right_logical(packed, 10 * part) & 1023 for part in range(3)]
            sources = starts + [starts[0] + 1 + half * (starts[1] - starts[0])]
            pieces.append(jnp.concatenate([whole[source] for source in sources], axis=1))
        picked = jnp.concatenate(pieces, axis=0)
        product = lax.dot_general(
            proj_ref[...], picked, (((1,), (1,)), ((), ())), preferred_element_type=jnp.float32
        )
        cols = pl.ds(pl.multiple_of(t * tile, tile), tile)
        update_ref[:, cols] = product.astype(jnp.bfloat16)
        pltpu.make_async_copy(update_ref.at[:, cols], update_hbm.at[:, cols], out_sem.at[t]).start()

    for copy in stores + passing:
        copy.wait()


def in_hbm(array):
    return pltpu.with_memory_space_constraint(array, pltpu.HBM)


def in_vmem(array):
    return pltpu.with_memory_space_constraint(array, pltpu.VMEM)


def local(gradients, projection, plan, first_codes, first_scales, second_codes, second_scales):
    panel_count = plan.shape[0]
    position = jnp.arange(panel_count, dtype=jnp.int32)
    owner = position // 2
    half = position % 2
    chip = {"x": owner // 32, "z": owner // 8 % RING, "y": owner // 2 % RING}
    base = (owner % 2) * HALF_ROWS
    starts = [
        (base + jnp.where(half == 0, block_row(0, part, chip), block_row(1, part, chip))) // PW for part in range(3)
    ]
    packed = starts[0] + starts[1] * 1024 + starts[2] * 1024 * 1024 + half * 1024 * 1024 * 1024
    found = plan[None, :] == position[:, None]
    table = jnp.sum(jnp.where(found, packed[None, :], 0), axis=1)

    bf16, f32 = jnp.bfloat16, jnp.float32
    vmem = pl.BlockSpec(memory_space=pltpu.VMEM)
    smem = pl.BlockSpec(memory_space=pltpu.SMEM)
    hbm = pl.BlockSpec(memory_space=pltpu.HBM)
    sem = pltpu.SemaphoreType.DMA
    rows_count, col_count = gradients.shape[1:]
    half_cols = col_count // 2
    whole, *moments = pl.pallas_call(
        kernel,
        out_shape=(
            pltpu.VMEM((2 * HALF_ROWS // PW, PW, LANES), bf16),
            pltpu.VMEM((first_codes.shape), bf16),
            pltpu.VMEM((first_scales.shape[::-1]), f32),
            pltpu.VMEM((second_codes.shape), bf16),
            pltpu.VMEM((second_scales.shape[::-1]), f32),
        ),
        in_specs=[smem] + [hbm] * 6,
        out_specs=(vmem, vmem, vmem, vmem, vmem),
        scratch_shapes=[
            pltpu.VMEM(projection.shape, bf16),
            pltpu.VMEM(first_codes.shape, bf16),
            pltpu.VMEM(first_scales.shape[::-1], f32),
            pltpu.VMEM(second_codes.shape, bf16),
            pltpu.VMEM(second_scales.shape[::-1], f32),
            pltpu.VMEM((rows_count, col_count), bf16),
            pltpu.VMEM((col_count // PW, PW, rows_count), bf16),
            pltpu.VMEM((half_cols, rows_count), bf16),
            pltpu.VMEM((half_cols, rows_count), bf16),
            pltpu.VMEM((half_cols, rows_count), bf16),
            pltpu.VMEM(projection.shape, bf16),
            pltpu.VMEM((HALF_ROWS, LANES), bf16),
            pltpu.VMEM((HALF_ROWS // 4, LANES), bf16),
            pltpu.VMEM((HALF_ROWS // 2, LANES), bf16),
            pltpu.VMEM((HALF_ROWS // 4, LANES), bf16),
            pltpu.VMEM((HALF_ROWS * 3 // 16, LANES), bf16),
            pltpu.VMEM((HALF_ROWS // 16, LANES), bf16),
            pltpu.VMEM((HALF_ROWS * 3 // 64, LANES), bf16),
            sem((4,)), sem((5,)), sem((3,)), sem((3,)), sem((36,)), sem((36,)), sem((36,)), sem((36,)), sem((36,)), sem((36,)),
            sem((36,)), sem((36,)), sem((42,)), sem((42,)),
        ],
        compiler_params=pltpu.CompilerParams(
            collective_id=0, has_side_effects=True, vmem_limit_bytes=54 * 1024 * 1024
        ),
    )(plan, *map(in_hbm, (gradients, projection, first_codes, first_scales.T, second_codes, second_scales.T)))
    update, first_out, first_peak, second_out, second_peak = pl.pallas_call(
        finish,
        out_shape=[jax.ShapeDtypeStruct((rows_count, col_count), bf16)]
        + [jax.ShapeDtypeStruct(moment.shape, moment.dtype) for moment in moments],
        in_specs=[smem, vmem, hbm] + [vmem] * 4,
        out_specs=[hbm] * 5,
        scratch_shapes=[
            pltpu.VMEM(projection.shape, bf16),
            pltpu.VMEM((2048, RANK), bf16),
            pltpu.VMEM((rows_count, col_count), bf16),
            sem((col_count // 2048,)),
            sem((4,)),
            sem,
        ],
        compiler_params=pltpu.CompilerParams(vmem_limit_bytes=24 * 1024 * 1024),
    )(table, in_vmem(whole), in_hbm(projection), *map(in_vmem, moments))
    return update, first_out, first_peak.T, second_out, second_peak.T


def solution(mesh):
    in_specs = (
        P("replica", "fsdp", None),
        P("fsdp", None),
        P(),
        P(("replica", "fsdp"), None),
        P(("replica", "fsdp"), None),
        P(("replica", "fsdp"), None),
        P(("replica", "fsdp"), None),
    )
    out_specs = (
        P("fsdp", None),
        P(("replica", "fsdp"), None),
        P(("replica", "fsdp"), None),
        P(("replica", "fsdp"), None),
        P(("replica", "fsdp"), None),
    )
    return jax.shard_map(local, mesh=mesh, in_specs=in_specs, out_specs=out_specs, check_vma=False)
```

```python
import functools

import jax
import jax.numpy as jnp
from jax import lax
from jax.experimental import pallas as pl
from jax.experimental.pallas import tpu as pltpu
from jax.sharding import PartitionSpec as P

PW = 32
QB = 256
STEP = 2
RING = 4
LANES = 128

beta_one = 0.9
beta_two = 0.999
adam_eps = 1e-08
scale_eps = 1e-06

MESH = pl.DeviceIdType.MESH

CHIPS = RING**3
OWNED = 64
RANK = 512
HALF_ROWS = 256 * CHIPS
ORDERS = (("x", "y", "z"), ("y", "z", "x"), ("z", "x", "y"))
LANES_OF = (((0, 3), (1,), (2,)), ((0,), (1, 3), (2,)))
BOTH = [(half, part) for half in range(2) for part in range(3)]


def part_of(half, part):
    sizes = [PW * len(lanes) for lanes in LANES_OF[half]]
    return ORDERS[part], sizes[part], half * HALF_ROWS // 2 + sum(sizes[:part]) * CHIPS


def block_row(half, part, chip):
    order, size, base = part_of(half, part)
    a, b, c = (chip[name] for name in order)
    return base + ((a * RING + b) * RING + c) * size


def shifted(chip, axis, step):
    moved = dict(chip)
    moved[axis] = lax.rem(chip[axis] + step, RING)
    return moved


def device_of(chip, core):
    return (chip["x"], (chip["z"] * RING + chip["y"]) * 2 + core)


def rows(start, size):
    return pl.ds(pl.multiple_of(start, 32), size)


def lanes_at(block):
    return slice(block * LANES, (block + 1) * LANES)


def kernel(
    plan_ref, grad_hbm, proj_hbm, fc_hbm, fs_hbm, sc_hbm, ss_hbm,
    whole, ofc_ref, ofs_ref, osc_ref, oss_ref,
    proj_ref, fc_ref, fs_ref, sc_ref, ss_ref, grad_ref, turned, other_out, other_in, own_rows, proj_other,
    sums1, transit, recv1, sums2, recv2, sums3, recv3,
    grad_sem, small_sem, pair_send, pair_recv, first_send, first_recv, rs_send, rs_recv, near_send, near_recv, ag_send, ag_recv, fwd_send, fwd_recv,
):
    replica = lax.axis_index("replica")
    inner = lax.axis_index("fsdp")
    chip = {"x": replica, "z": inner // 8, "y": lax.rem(inner // 2, RING)}
    core = lax.rem(inner, 2)
    other = 1 - core
    sibling = device_of(chip, other)
    cols = grad_hbm.shape[2] // RING

    loads = []
    for j in range(RING):
        loads.append(
            pltpu.make_async_copy(
                grad_hbm.at[0, :, pl.ds(j * cols, cols)], grad_ref.at[:, pl.ds(j * cols, cols)], grad_sem.at[j]
            )
        )
        loads[-1].start()

    small = []
    for i, (source, target) in enumerate(
        ((proj_hbm, proj_ref), (fc_hbm, fc_ref), (fs_hbm, fs_ref), (sc_hbm, sc_ref), (ss_hbm, ss_ref))
    ):
        small.append(pltpu.make_async_copy(source, target, small_sem.at[i]))
        small[-1].start()

    barrier = pltpu.get_barrier_semaphore()
    pl.semaphore_signal(barrier, inc=1, device_id=sibling, device_id_type=MESH)
    for axis in ("x", "y", "z"):
        for step in range(1, RING):
            pl.semaphore_signal(
                barrier, inc=1, device_id=device_of(shifted(chip, axis, step), core), device_id_type=MESH
            )

    for j in range(RING):
        loads[j].wait()

        @pl.loop(0, cols // 256)
        def _(t, j=j):
            at = pl.multiple_of(j * cols + t * 256, 256)
            block = grad_ref[:, pl.ds(at, 256)].T
            turned[pl.ds(at // PW, 256 // PW)] = block.reshape(256 // PW, PW, block.shape[1])

    for copy in small:
        copy.wait()
    pl.semaphore_wait(barrier, 3 * (RING - 1) + 1)

    def remote(src, dst, send, recv, target):
        return pltpu.make_async_remote_copy(
            src_ref=src, dst_ref=dst, send_sem=send, recv_sem=recv, device_id=target, device_id_type=MESH
        )

    proj_copy = remote(proj_ref, proj_other, pair_send.at[2], pair_recv.at[2], sibling)
    proj_copy.start()

    span = CHIPS * PW

    def pick(target, which, half):
        @pl.loop(0, CHIPS)
        def _(t):
            target[rows(half * span + t * PW, PW), :] = turned[plan_ref[(t * 2 + which) * 2 + half]]

    pair = []
    for half in range(2):
        pick(other_out, other, half)
        part_rows = pl.ds(half * span, span)
        pair.append(
            remote(
                other_out.at[part_rows, :], other_in.at[part_rows, :],
                pair_send.at[half], pair_recv.at[half], sibling,
            )
        )
        pair[-1].start()

    def project(half):
        pick(own_rows, core, half)
        if half == 0:
            proj_copy.wait_recv()
        pair[half].wait_recv()

        @pl.loop(0, CHIPS // 8)
        def _(t):
            at = rows(half * span + t * 8 * PW, 8 * PW)
            product = jnp.dot(own_rows[at, :], proj_ref[...], preferred_element_type=jnp.float32)
            product += jnp.dot(other_in[at, :], proj_other[...], preferred_element_type=jnp.float32)
            for i in range(8):
                to = {"x": t // 2, "z": (t % 2) * 2 + i // 4, "y": i % 4}
                for part in range(3):
                    for j, block in enumerate(LANES_OF[half][part]):
                        sums1[rows(block_row(half, part, to) + j * PW, PW), :] = product[
                            i * PW : (i + 1) * PW, lanes_at(block)
                        ].astype(jnp.bfloat16)

    def sub_row(half, part, a, b):
        order = ORDERS[part]
        return block_row(half, part, {order[0]: a, order[1]: b, order[2]: 0})

    opening, middle, closing = {}, {}, {}
    for half, part in BOTH:
        order, size, base = part_of(half, part)
        a = chip[order[0]]
        message = 2 * size * RING
        for way, flow in enumerate((1, RING - 1)):
            onward = device_of(shifted(chip, order[0], flow), core)
            backward = device_of(shifted(chip, order[0], RING - flow), core)
            sem = half * 6 + part * 2 + way
            land = base // 2 + way * 2 * message
            for kind, (steps, landing, place, target) in enumerate(
                (
                    (2, transit, base // 4 + way * message, onward),
                    (RING - flow, recv1, land, backward),
                    (flow, recv1, land + message, onward),
                )
            ):
                opening[kind, half, part, way] = remote(
                    sums1.at[rows(sub_row(half, part, lax.rem(a + steps, RING), 2 * way), message), :],
                    landing.at[pl.ds(place, message), :],
                    first_send.at[12 * kind + sem], first_recv.at[12 * kind + sem], target,
                )
        for stage, source, landing, copies in ((1, sums2, recv2, middle), (2, sums3, recv3, closing)):
            unit = size * RING ** (2 - stage)
            origin = base // RING**stage
            for step in range(1, RING):
                to = shifted(chip, order[stage], step)
                sem = (stage - 1) * 18 + half * 9 + part * 3 + step - 1
                copies[half, part, step] = remote(
                    source.at[rows(origin + to[order[stage]] * unit, unit), :],
                    landing.at[pl.ds(3 * base // RING ** (stage + 1) + (step - 1) * unit, unit), :],
                    rs_send.at[sem], rs_recv.at[sem], device_of(to, core),
                )

    def opening_start(kind, half):
        for part in range(3):
            for way in range(2):
                opening[kind, half, part, way].start()

    def add(count, target, at, *terms):
        tile = 128

        @pl.loop(0, count // tile)
        def _(t):
            total = sum(ref[rows(row + t * tile, tile), :].astype(jnp.float32) for ref, row in terms)
            target[rows(at + t * tile, tile), :] = total.astype(jnp.bfloat16)

    def pass_on(half):
        for part in range(3):
            order, size, base = part_of(half, part)
            message = 2 * size * RING
            for way, flow in enumerate((1, RING - 1)):
                opening[0, half, part, way].wait_recv()
                own = sub_row(half, part, lax.rem(chip[order[0]] + flow, RING), 2 * way)
                add(message, sums1, own, (sums1, own), (transit, base // 4 + way * message))
                opening[2, half, part, way].start()

    def first_done(half):
        for part in range(3):
            order, size, base = part_of(half, part)
            message = 2 * size * RING
            for way in range(2):
                opening[1, half, part, way].wait_recv()
                opening[2, half, part, way].wait_recv()
                own = sub_row(half, part, chip[order[0]], 2 * way)
                land = base // 2 + way * 2 * message
                add(
                    message, sums2, base // RING + way * message,
                    (sums1, own), (recv1, land), (recv1, land + message),
                )
            for step in (2, 1, 3):
                middle[half, part, step].start()

    def middle_done(half):
        for part in range(3):
            order, size, base = part_of(half, part)
            for step in range(1, RING):
                middle[half, part, step].wait_recv()
            unit = size * RING
            own = base // RING + chip[order[1]] * unit
            landings = [(recv2, 3 * base // RING**2 + i * unit) for i in range(3)]
            add(unit, sums3, base // RING**2, (sums2, own), *landings)
            for step in (2, 1, 3):
                closing[half, part, step].start()

    first_scales, second_scales = fs_ref[...].T, ss_ref[...].T
    peaks = ([], [])

    def adam(half):
        low = {}
        for part in range(3):
            order, size, base = part_of(half, part)
            for step in range(1, RING):
                closing[half, part, step].wait_recv()
            total = sums3[rows(base // 16 + chip[order[2]] * size, size), :].astype(jnp.float32)
            for i in range(3):
                total += recv3[pl.ds(3 * base // 64 + i * size, size), :].astype(jnp.float32)
            for j, block in enumerate(LANES_OF[half][part]):
                low[block] = total[j * PW : (j + 1) * PW, :]
        row = slice(half * PW, (half + 1) * PW)
        mine_peaks = ([], [])
        direction = {}
        for b in range(RANK // QB):
            lane = slice(b * QB, (b + 1) * QB)
            lowrank = jnp.concatenate([low[2 * b], low[2 * b + 1]], axis=1)
            first = fc_ref[row, lane].astype(jnp.float32) * first_scales[row, b : b + 1]
            second = sc_ref[row, lane].astype(jnp.float32) * second_scales[row, b : b + 1]
            first_new = beta_one * first + (1.0 - beta_one) * lowrank
            second_new = beta_two * second + (1.0 - beta_two) * lowrank * lowrank
            corr_one = 1.0 - beta_one**STEP
            corr_two = 1.0 - beta_two**STEP
            result = (first_new / corr_one / (jnp.sqrt(second_new / corr_two) + adam_eps)).astype(jnp.bfloat16)
            for i in range(2):
                direction[2 * b + i] = result[:, lanes_at(i)]
            for i, (value, codes) in enumerate(((first_new, ofc_ref), (second_new, osc_ref))):
                peak = jnp.max(jnp.abs(value), axis=1, keepdims=True) + scale_eps
                codes[row, lane] = (value / peak).astype(jnp.bfloat16)
                mine_peaks[i].append(peak)
        for i in range(2):
            peaks[i].append(jnp.concatenate(mine_peaks[i], axis=1))
        for part in range(3):
            at = (mine + block_row(half, part, chip)) // PW
            for j, block in enumerate(LANES_OF[half][part]):
                whole[at + j] = direction[block]

    mine, theirs = core * HALF_ROWS, other * HALF_ROWS
    started, forwards = [], []

    def copy_of(start, size, send, recv, target):
        where = whole.at[pl.ds(start // PW, size // PW)]
        return remote(where, where, send, recv, target)

    def spread(start, size, send, recv, target):
        started.append(copy_of(mine + start, size, send, recv, target))
        started[-1].start()

    def forward(start, size):
        index = len(forwards)
        forwards.append((start, size))
        spread(start, size, fwd_send.at[index], fwd_recv.at[index], sibling)

    def landed(start, size, recv):
        copy_of(mine + start, size, first_send.at[0], recv, sibling).wait_recv()
        return start, size

    def direct_start(stage, half):
        for part in range(3):
            order, size, base = part_of(half, part)
            if stage == 2:
                piece = block_row(half, part, chip), size
            else:
                for step in range(1, RING):
                    start = block_row(half, part, shifted(chip, order[2], RING - step))
                    landed(start, size, ag_recv.at[18 + half * 9 + part * 3 + step - 1])
                piece = sub_row(half, part, chip[order[0]], chip[order[1]]), size * RING
            for step in (2, 1, 3):
                sem = (stage - 1) * 18 + half * 9 + part * 3 + step - 1
                to = device_of(shifted(chip, order[stage], step), core)
                spread(*piece, ag_send.at[sem], ag_recv.at[sem], to)

    def wide_piece(half, part, a_off, way):
        order, size, base = part_of(half, part)
        return sub_row(half, part, lax.rem(chip[order[0]] + a_off, RING), 2 * way), 2 * size * RING

    def near_start(half):
        for part in range(3):
            order, size, base = part_of(half, part)
            for step in range(1, RING):
                start = sub_row(half, part, chip[order[0]], lax.rem(chip[order[1]] + RING - step, RING))
                landed(start, size * RING, ag_recv.at[half * 9 + part * 3 + step - 1])
            for turn in range(2):
                for way, flow in enumerate((1, RING - 1)):
                    content = way ^ turn
                    sem = half * 12 + part * 4 + way * 2 + content
                    to = device_of(shifted(chip, order[0], flow), core)
                    spread(*wide_piece(half, part, 0, content), near_send.at[sem], near_recv.at[sem], to)
            forward(sub_row(half, part, chip[order[0]], 0), size * RING * RING)

    def near_landed(half, turn):
        for part in range(3):
            order = ORDERS[part]
            for way, flow in enumerate((1, RING - 1)):
                content = way ^ turn
                piece = landed(
                    *wide_piece(half, part, RING - flow, content),
                    near_recv.at[half * 12 + part * 4 + way * 2 + content],
                )
                if turn == 0:
                    sem = 24 + half * 6 + part * 2 + way
                    to = device_of(shifted(chip, order[0], flow), core)
                    spread(*piece, near_send.at[sem], near_recv.at[sem], to)
                forward(*piece)

    def far_landed(half):
        for part in range(3):
            for way in range(2):
                forward(*landed(*wide_piece(half, part, 2, way), near_recv.at[24 + half * 6 + part * 2 + way]))

    project(0)
    opening_start(0, 0)
    opening_start(1, 0)
    project(1)
    opening_start(0, 1)
    pass_on(0)
    opening_start(1, 1)
    pass_on(1)
    first_done(0)
    first_done(1)
    middle_done(0)
    adam(0)
    direct_start(2, 0)
    middle_done(1)
    direct_start(1, 0)
    adam(1)
    direct_start(2, 1)
    near_start(0)
    direct_start(1, 1)
    near_start(1)
    for turn in range(2):
        for half in range(2):
            near_landed(half, turn)
    far_landed(0)
    far_landed(1)
    ofs_ref[...] = jnp.concatenate(peaks[0], axis=0).T
    oss_ref[...] = jnp.concatenate(peaks[1], axis=0).T
    for index, (start, size) in enumerate(forwards):
        copy_of(theirs + start, size, first_send.at[0], fwd_recv.at[index], sibling).wait_recv()

    proj_copy.wait_send()
    for copy in pair:
        copy.wait_send()
    for stage in (opening, middle, closing):
        for copy in stage.values():
            copy.wait_send()
    for copy in started:
        copy.wait_send()


def finish(table_ref, whole, proj_ref, *refs):
    passed, update_hbm, outs = refs[:4], refs[4], refs[5:9]
    natural, update_ref, out_sem, pass_sem = refs[9:]
    passing = [pltpu.make_async_copy(passed[i], outs[i], pass_sem.at[i]) for i in range(4)]
    for copy in passing:
        copy.start()
    tile = natural.shape[0]
    steps = update_ref.shape[1] // tile
    stores = []
    for t in range(steps):
        cols = pl.ds(t * tile, tile)
        stores.append(pltpu.make_async_copy(update_ref.at[:, cols], update_hbm.at[:, cols], out_sem.at[t]))

    @pl.loop(0, steps)
    def _(t):
        pieces = []
        for p in range(tile // PW):
            packed = table_ref[t * (tile // PW) + p]
            half = lax.shift_right_logical(packed, 30)
            starts = [lax.shift_right_logical(packed, 10 * part) & 1023 for part in range(3)]
            sources = starts + [starts[0] + 1 + half * (starts[1] - starts[0])]
            pieces.append(jnp.concatenate([whole[source] for source in sources], axis=1))
        picked = jnp.concatenate(pieces, axis=0)
        product = lax.dot_general(
            proj_ref[...], picked, (((1,), (1,)), ((), ())), preferred_element_type=jnp.float32
        )
        cols = pl.ds(pl.multiple_of(t * tile, tile), tile)
        update_ref[:, cols] = product.astype(jnp.bfloat16)
        pltpu.make_async_copy(update_ref.at[:, cols], update_hbm.at[:, cols], out_sem.at[t]).start()

    for copy in stores + passing:
        copy.wait()


def in_hbm(array):
    return pltpu.with_memory_space_constraint(array, pltpu.HBM)


def in_vmem(array):
    return pltpu.with_memory_space_constraint(array, pltpu.VMEM)


def local(gradients, projection, plan, first_codes, first_scales, second_codes, second_scales):
    panel_count = plan.shape[0]
    position = jnp.arange(panel_count, dtype=jnp.int32)
    owner = position // 2
    half = position % 2
    chip = {"x": owner // 32, "z": owner // 8 % RING, "y": owner // 2 % RING}
    base = (owner % 2) * HALF_ROWS
    starts = [
        (base + jnp.where(half == 0, block_row(0, part, chip), block_row(1, part, chip))) // PW for part in range(3)
    ]
    packed = starts[0] + starts[1] * 1024 + starts[2] * 1024 * 1024 + half * 1024 * 1024 * 1024
    found = plan[None, :] == position[:, None]
    table = jnp.sum(jnp.where(found, packed[None, :], 0), axis=1)

    bf16, f32 = jnp.bfloat16, jnp.float32
    vmem = pl.BlockSpec(memory_space=pltpu.VMEM)
    smem = pl.BlockSpec(memory_space=pltpu.SMEM)
    hbm = pl.BlockSpec(memory_space=pltpu.HBM)
    sem = pltpu.SemaphoreType.DMA
    rows_count, col_count = gradients.shape[1:]
    half_cols = col_count // 2
    whole, *moments = pl.pallas_call(
        kernel,
        out_shape=(
            pltpu.VMEM((2 * HALF_ROWS // PW, PW, LANES), bf16),
            pltpu.VMEM((first_codes.shape), bf16),
            pltpu.VMEM((first_scales.shape[::-1]), f32),
            pltpu.VMEM((second_codes.shape), bf16),
            pltpu.VMEM((second_scales.shape[::-1]), f32),
        ),
        in_specs=[smem] + [hbm] * 6,
        out_specs=(vmem, vmem, vmem, vmem, vmem),
        scratch_shapes=[
            pltpu.VMEM(projection.shape, bf16),
            pltpu.VMEM(first_codes.shape, bf16),
            pltpu.VMEM(first_scales.shape[::-1], f32),
            pltpu.VMEM(second_codes.shape, bf16),
            pltpu.VMEM(second_scales.shape[::-1], f32),
            pltpu.VMEM((rows_count, col_count), bf16),
            pltpu.VMEM((col_count // PW, PW, rows_count), bf16),
            pltpu.VMEM((half_cols, rows_count), bf16),
            pltpu.VMEM((half_cols, rows_count), bf16),
            pltpu.VMEM((half_cols, rows_count), bf16),
            pltpu.VMEM(projection.shape, bf16),
            pltpu.VMEM((HALF_ROWS, LANES), bf16),
            pltpu.VMEM((HALF_ROWS // 4, LANES), bf16),
            pltpu.VMEM((HALF_ROWS // 2, LANES), bf16),
            pltpu.VMEM((HALF_ROWS // 4, LANES), bf16),
            pltpu.VMEM((HALF_ROWS * 3 // 16, LANES), bf16),
            pltpu.VMEM((HALF_ROWS // 16, LANES), bf16),
            pltpu.VMEM((HALF_ROWS * 3 // 64, LANES), bf16),
            sem((4,)), sem((5,)), sem((3,)), sem((3,)), sem((36,)), sem((36,)), sem((36,)), sem((36,)), sem((36,)), sem((36,)),
            sem((36,)), sem((36,)), sem((42,)), sem((42,)),
        ],
        compiler_params=pltpu.CompilerParams(
            collective_id=0, has_side_effects=True, vmem_limit_bytes=54 * 1024 * 1024
        ),
    )(plan, *map(in_hbm, (gradients, projection, first_codes, first_scales.T, second_codes, second_scales.T)))
    update, first_out, first_peak, second_out, second_peak = pl.pallas_call(
        finish,
        out_shape=[jax.ShapeDtypeStruct((rows_count, col_count), bf16)]
        + [jax.ShapeDtypeStruct(moment.shape, moment.dtype) for moment in moments],
        in_specs=[smem, vmem, vmem] + [vmem] * 4,
        out_specs=[hbm] * 5,
        scratch_shapes=[
            pltpu.VMEM((2048, RANK), bf16),
            pltpu.VMEM((rows_count, col_count), bf16),
            sem((col_count // 2048,)),
            sem((4,)),
        ],
        compiler_params=pltpu.CompilerParams(vmem_limit_bytes=24 * 1024 * 1024),
    )(table, in_vmem(whole), in_vmem(projection), *map(in_vmem, moments))
    return update, first_out, first_peak.T, second_out, second_peak.T


def solution(mesh):
    in_specs = (
        P("replica", "fsdp", None),
        P("fsdp", None),
        P(),
        P(("replica", "fsdp"), None),
        P(("replica", "fsdp"), None),
        P(("replica", "fsdp"), None),
        P(("replica", "fsdp"), None),
    )
    out_specs = (
        P("fsdp", None),
        P(("replica", "fsdp"), None),
        P(("replica", "fsdp"), None),
        P(("replica", "fsdp"), None),
        P(("replica", "fsdp"), None),
    )
    return jax.shard_map(local, mesh=mesh, in_specs=in_specs, out_specs=out_specs, check_vma=False)
```
